32 devices in a mesh: rep: 8 (over z, y), gx: 2 (over x), gy: 2 (over core).
Axes of the slice: x: 2, y: 2, z: 4, core: 2. Of those that a mesh axis runs over, the one named last changes fastest.
Arguments:
- particle_descriptors: bfloat16 [8, 4, 4, 128, 128], P('rep', 'gx', 'gy'), may hold values from -6 to 6
- particle_locations_all: float32 [8, 3, 4, 4, 128], P('rep', None, 'gx', 'gy'), may hold values from 0 to 4, as said below
- earlier_jitter: float32 [8, 3, 4, 4, 128], P('rep', None, 'gx', 'gy'), may hold values from -6 to 6
- later_jitter: float32 [8, 3, 4, 4, 128], P('rep', None, 'gx', 'gy'), may hold values from -6 to 6
- adjacent_tile_slots: int32 [4, 4, 6], P('gx', 'gy'), may hold values from -1 to 15, as said below
- thermal_levels: float32 [8], replicated, may hold values from 0.5 to 2
- heat_slot_of_copy: int32 [8], P('rep'), may hold values from 0 to 7, as said below
- partner_choice: int32 [8], replicated, may hold values from 0 to 7, as said below
- normalizer_gain: float32 [128], replicated, may hold values from 0.25 to 1.75
- query_lookup_matrix: bfloat16 [128, 384], replicated, may hold values from -0.5 to 0.5
- message_output_matrix: bfloat16 [128, 128], replicated, may hold values from -0.5 to 0.5
- lookup_charge_map: bfloat16 [128], replicated, may hold values from -0.5 to 0.5
- attention_head_falloff: float32 [8], replicated, may hold values from 0.5 to 8
- attention_head_weight: float32 [8], replicated, may hold values from -4 to 4
Outputs:
- interval_descriptors: bfloat16 [8, 4, 4, 128, 128], P('rep', 'gx', 'gy')
- interval_locations: float32 [8, 3, 4, 4, 128], P('rep', None, 'gx', 'gy')
- later_pulls: float32 [8, 3, 4, 4, 128], P('rep', None, 'gx', 'gy')
The draws below stay inside these ranges and needn't reach their ends.
Inputs may be any that keep to these rules, and one draw needn't show every extreme that they name: `adjacent_tile_slots`: each tile's first slot names the tile itself; the others name distinct tiles of the 3 x 3 block of tiles around it that lie inside the grid, as row-major indices into the device's block of tiles extended by one tile on each side (4 columns); -1 marks an empty slot, and empty slots come last. `heat_slot_of_copy`: A permutation. `partner_choice`: an involution: each replica takes its own configuration or that of the replica whose temperature slot is next to its own. `particle_locations_all`: for a bead of the tile at grid position (a, b) the first coordinate lies in [a, a + 1], the second in [b, b + 1], the third in [0, 1].
All inputs are finite; a program needn't handle non-finite values.
Results may differ from the reference program's by a relative error of at most 0.0091.
Values may be sent and summed in bfloat16 or wider, within the bound.
A program may use at most 64 MiB of HBM per device.

```python
import math
import jax
import jax.numpy as jnp
from jax import lax

F = 128
HEADS = 8
TILE = 128
K = 6
TX = 2
TY = 2
NREP = 8
GTX = 4
GTY = 4


def draw_particle_locations_all(key, part):
    array_shape = (NREP, 3, GTX, GTY, TILE)
    fraction = jax.random.uniform(key, array_shape, jnp.float32)
    component = jnp.arange(3)[None, :, None, None, None]
    grid_row = jnp.arange(GTX, dtype=jnp.float32)[None, None, :, None, None]
    grid_col = jnp.arange(GTY, dtype=jnp.float32)[None, None, None, :, None]
    anchor = jnp.where(component == 0, grid_row, jnp.where(component == 1, grid_col, 0.0))
    return anchor + fraction


def draw_adjacent_tile_slots(key, part):
    step_row = jnp.array([-1, -1, -1, 0, 0, 1, 1, 1], dtype=jnp.int32)
    step_col = jnp.array([-1, 0, 1, -1, 1, -1, 0, 1], dtype=jnp.int32)
    grid_row = jnp.arange(GTX, dtype=jnp.int32)[:, None, None]
    grid_col = jnp.arange(GTY, dtype=jnp.int32)[None, :, None]
    target_row = grid_row + step_row
    target_col = grid_col + step_col
    inside = (target_row >= 0) & (target_row < GTX) & (target_col >= 0) & (target_col < GTY)
    ranking = jax.random.randint(key, (GTX, GTY, 8), 0, 2 ** 20, dtype=jnp.int32) * 16 + jnp.arange(8, dtype=jnp.int32)
    ranking = jnp.where(inside, ranking, ranking + 2 ** 26)
    picked = jnp.argsort(ranking, axis=-1)[..., :K - 1]
    chosen_row = step_row[picked]
    chosen_col = step_col[picked]
    chosen_inside = jnp.take_along_axis(inside, picked, axis=-1)
    local_row = grid_row % TX + 1
    local_col = grid_col % TY + 1
    others = (local_row + chosen_row) * (TY + 2) + local_col + chosen_col
    others = jnp.where(chosen_inside, others, -1)
    itself = jnp.broadcast_to(local_row * (TY + 2) + local_col, (GTX, GTY, 1))
    return jnp.concatenate([itself, others], axis=-1).astype(jnp.int32)


def replica_ladder(key):
    base_key = jax.random.fold_in(key, 31)
    first_key, second_key, third_key = jax.random.split(base_key, 3)
    slot_of = jax.random.permutation(first_key, NREP).astype(jnp.int32)
    holder = jnp.argsort(slot_of).astype(jnp.int32)
    parity = jax.random.randint(second_key, (), 0, 2, dtype=jnp.int32)
    accepted = jax.random.randint(third_key, (NREP,), 0, 4, dtype=jnp.int32) > 0
    slot_ids = jnp.arange(NREP, dtype=jnp.int32)
    shifted = slot_ids - parity
    goes_up = (shifted >= 0) & (shifted % 2 == 0) & (slot_ids + 1 < NREP)
    goes_down = (shifted >= 1) & (shifted % 2 == 1)
    pair_number = jnp.clip(jnp.where(goes_up, shifted // 2, (shifted - 1) // 2), 0, NREP - 1)
    accepted_pair = accepted[pair_number]
    partner = jnp.where(goes_up & accepted_pair, slot_ids + 1, jnp.where(goes_down & accepted_pair, slot_ids - 1, slot_ids))
    return (slot_of, holder[partner[slot_of]].astype(jnp.int32))


def draw_heat_slot_of_copy(key, part):
    slot_of, partners = replica_ladder(key)
    return slot_of


def draw_partner_choice(key, part):
    slot_of, partners = replica_ladder(key)
    return partners


def levels(stream_key, extent, cuts, low, largest):
    def one(dim, parts):
        heights = jax.random.uniform(jax.random.fold_in(jax.random.fold_in(stream_key, 6), dim), (parts,), jnp.float32, low / len(cuts), largest / len(cuts))
        return jnp.repeat(jnp.exp(heights), extent[dim] // parts).reshape((-1,) + (1,) * (len(extent) - dim - 1))

    loudness = one(*cuts[0])
    for cut in cuts[1:]:
        loudness = loudness * one(*cut)
    return loudness


def normal_values(key, shape, deviation, limit, shards=(), kind=jnp.bfloat16):
    loudness = levels(key, shape, shards, -0.22, 0.18) if shards else 1.0
    entries = jax.random.normal(key, shape, jnp.float32) * deviation * loudness
    return jnp.minimum(jnp.maximum(entries, -limit), limit).astype(kind)


def setup_inputs(seed: int = 0) -> dict:
    keys = jax.random.split(jax.random.key(seed), 15)
    return {
        "particle_descriptors": normal_values(keys[0], (NREP, GTX, GTY, TILE, F), 1.0, 6.0, ((0, 8), (1, 2), (2, 2))),
        "particle_locations_all": draw_particle_locations_all(jax.random.fold_in(keys[14], 71), 0),
        "earlier_jitter": normal_values(keys[2], (NREP, 3, GTX, GTY, TILE), 1.0, 6.0, ((0, 8), (2, 2), (3, 2)), jnp.float32),
        "later_jitter": normal_values(keys[3], (NREP, 3, GTX, GTY, TILE), 1.0, 6.0, ((0, 8), (2, 2), (3, 2)), jnp.float32),
        "adjacent_tile_slots": draw_adjacent_tile_slots(jax.random.fold_in(keys[14], 71), 0),
        "thermal_levels": jnp.clip(jnp.exp(jax.random.uniform(keys[5], (NREP,), jnp.float32, math.log(0.5), math.log(2.0))), 0.5, 2.0),
        "heat_slot_of_copy": draw_heat_slot_of_copy(jax.random.fold_in(keys[14], 71), 0),
        "partner_choice": draw_partner_choice(jax.random.fold_in(keys[14], 71), 0),
        "normalizer_gain": jnp.clip(1.0 + 0.15 * jax.random.normal(keys[8], (F,), jnp.float32), 0.25, 1.75),
        "query_lookup_matrix": normal_values(keys[9], (F, 3 * F), F ** -0.5, 0.5),
        "message_output_matrix": normal_values(keys[10], (F, F), F ** -0.5, 0.5),
        "lookup_charge_map": normal_values(keys[11], (F,), F ** -0.5, 0.5),
        "attention_head_falloff": jnp.clip(jnp.exp(jax.random.uniform(keys[12], (HEADS,), jnp.float32, math.log(0.5), math.log(8.0))), 0.5, 8.0),
        "attention_head_weight": normal_values(keys[13], (HEADS,), 1.0, 4.0, (), jnp.float32),
    }


NORM_EPS = 1e-05
DURATION_DELTA = 0.1
JITTER_SIZE = 0.05
MESSAGE_SCALE = 1.0 / 32.0
FORCE_SCALE = 1.0 / 16.0

def layer_norm(latent_vector, normalizer_gain):
    values = latent_vector.astype(jnp.float32)
    center = lax.optimization_barrier(jnp.mean(values, axis=-1, keepdims=True))
    spread = lax.optimization_barrier(jnp.mean((values - center) ** 2, axis=-1, keepdims=True))
    return ((values - center) * lax.rsqrt(spread + NORM_EPS) * normalizer_gain).astype(jnp.bfloat16)

def tile_terms(query_rows, own_coords, keyval, probe_values, near_coords, occupied_flags, attention_head_falloff, attention_head_weight):
    bead_count, feature_count = query_rows.shape
    head_count = attention_head_falloff.shape[0]
    head_size = feature_count // head_count
    slot_count = keyval.shape[0]
    queries = query_rows.astype(jnp.float32).reshape(bead_count, head_count, head_size)
    keys_heads = keyval[..., :feature_count].astype(jnp.float32).reshape(slot_count, bead_count, head_count, head_size)
    values_heads = keyval[..., feature_count:].astype(jnp.float32).reshape(slot_count, bead_count, head_count, head_size)
    logits = jnp.einsum('ihd,njhd->hinj', queries, keys_heads)
    offsets = own_coords[:, :, None, None] - near_coords[:, None, :, :]
    squared = lax.optimization_barrier(jnp.sum(offsets * offsets, axis=0))
    radius = jnp.sqrt(squared)
    envelope = jnp.where(radius < 1.0, 0.5 * (jnp.cos(jnp.pi * radius) + 1.0), 0.0)
    envelope = envelope * occupied_flags.astype(jnp.float32)[None, :, None]
    scores = jax.nn.silu(logits / math.sqrt(head_size)) * envelope[None] * jnp.exp(-attention_head_falloff[:, None, None, None] * squared[None])
    rounded = lax.optimization_barrier(scores.astype(jnp.bfloat16)).astype(jnp.float32)
    message = jnp.einsum('hinj,njhd->ihd', rounded, values_heads) * MESSAGE_SCALE
    message = message.reshape(bead_count, feature_count).astype(jnp.bfloat16)
    mixing = lax.optimization_barrier(jnp.sum(attention_head_weight[:, None, None, None] * scores, axis=0))
    particle_pulls = lax.optimization_barrier(jnp.sum(offsets * (mixing * probe_values[None, :, :])[None], axis=(2, 3))) * FORCE_SCALE
    return (message, particle_pulls)

def global_slots(adjacent_tile_slots):
    occupied_flags = adjacent_tile_slots >= 0
    clipped = jnp.maximum(adjacent_tile_slots, 0)
    grid_row = jnp.arange(GTX, dtype=jnp.int32)[:, None, None]
    grid_col = jnp.arange(GTY, dtype=jnp.int32)[None, :, None]
    padded_row = grid_row - grid_row % TX + clipped // (TY + 2)
    padded_col = grid_col - grid_col % TY + clipped % (TY + 2)
    linear_offset = (padded_row * (GTY + 2) + padded_col).astype(jnp.int32)
    return (linear_offset.reshape(-1, K), occupied_flags.reshape(-1, K))

def propagate_copy(latent_vector, particle_locations, stochastic_jolts, copy_heat_level, linear_offset, occupied_flags, network_weights):
    normalizer_gain, query_lookup_matrix, message_output_matrix, lookup_charge_map, attention_head_falloff, attention_head_weight = network_weights
    grid_rows, grid_cols, tile_beads, feature_count = latent_vector.shape
    normed = layer_norm(latent_vector, normalizer_gain)
    projected = jnp.dot(normed.reshape(-1, feature_count), query_lookup_matrix, preferred_element_type=jnp.float32).astype(jnp.bfloat16)
    query_rows = projected[:, :feature_count].reshape(-1, tile_beads, feature_count)
    keyval = projected[:, feature_count:].reshape(grid_rows, grid_cols, tile_beads, 2 * feature_count)
    keyval = jnp.pad(keyval, ((1, 1), (1, 1), (0, 0), (0, 0))).reshape(-1, tile_beads, 2 * feature_count)
    probe_values = jnp.dot(keyval[..., :feature_count].reshape(-1, feature_count), lookup_charge_map, preferred_element_type=jnp.float32).reshape(-1, tile_beads)
    near_coords = jnp.pad(particle_locations, ((0, 0), (1, 1), (1, 1), (0, 0))).reshape(3, -1, tile_beads)
    own_coords = particle_locations.reshape(3, -1, tile_beads).transpose(1, 0, 2)

    def per_tile(tile_item):
        tile_query, tile_coords, tile_slots, tile_present = tile_item
        return tile_terms(tile_query, tile_coords, keyval[tile_slots], probe_values[tile_slots], near_coords[:, tile_slots], tile_present, attention_head_falloff, attention_head_weight)
    message, particle_pulls = lax.map(per_tile, (query_rows, own_coords, linear_offset, occupied_flags))
    mixed = jnp.dot(message.reshape(-1, feature_count), message_output_matrix, preferred_element_type=jnp.float32).reshape(latent_vector.shape)
    revised_latent = (latent_vector.astype(jnp.float32) + mixed).astype(jnp.bfloat16)
    particle_pulls = particle_pulls.transpose(1, 0, 2).reshape(particle_locations.shape)
    moved_locations = particle_locations + DURATION_DELTA * particle_pulls + JITTER_SIZE * jnp.sqrt(copy_heat_level) * stochastic_jolts
    return (revised_latent, moved_locations, particle_pulls)

def reference(particle_descriptors, particle_locations_all, earlier_jitter, later_jitter, adjacent_tile_slots, thermal_levels, heat_slot_of_copy, partner_choice, normalizer_gain, query_lookup_matrix, message_output_matrix, lookup_charge_map, attention_head_falloff, attention_head_weight):
    network_weights = (normalizer_gain, query_lookup_matrix, message_output_matrix, lookup_charge_map, attention_head_falloff, attention_head_weight)
    linear_offset, occupied_flags = global_slots(adjacent_tile_slots)
    heat_level_series = jnp.take(thermal_levels, heat_slot_of_copy)

    def earlier_move(copy_element):
        latent_vector, particle_locations, stochastic_jolts, copy_heat_level = copy_element
        revised_latent, moved_locations, ignored_output = propagate_copy(latent_vector, particle_locations, stochastic_jolts, copy_heat_level, linear_offset, occupied_flags, network_weights)
        return (revised_latent, moved_locations)
    starting_latent, starting_locations = lax.map(earlier_move, (particle_descriptors, particle_locations_all, earlier_jitter, heat_level_series))
    traded_latent = jnp.take(starting_latent, partner_choice, axis=0)
    traded_locations = jnp.take(starting_locations, partner_choice, axis=0)

    def later_move(copy_element):
        latent_vector, particle_locations, stochastic_jolts, copy_heat_level = copy_element
        return propagate_copy(latent_vector, particle_locations, stochastic_jolts, copy_heat_level, linear_offset, occupied_flags, network_weights)
    interval_descriptors, interval_locations, later_pulls = lax.map(later_move, (traded_latent, traded_locations, later_jitter, heat_level_series))
    return (interval_descriptors, interval_locations, later_pulls)
```

```python
import functools
import math

import jax
import jax.numpy as jnp
from jax import lax
from jax.experimental import pallas as pl
from jax.experimental.pallas import tpu as pltpu
from jax.sharding import PartitionSpec as P

NORM_EPS = 1e-05
DURATION_DELTA = 0.1
JITTER_SIZE = 0.05
MESSAGE_SCALE = 1.0 / 32.0
FORCE_SCALE = 1.0 / 16.0
LOG2E = math.log2(math.e)


def window_coefficients(degree):
    import numpy as np

    nodes = 0.5 - 0.5 * np.cos(np.pi * (np.arange(64) + 0.5) / 64)
    target = np.cos(0.5 * np.pi * np.sqrt(nodes)) / (1.0 - nodes)
    return [float(c) for c in np.polyfit(nodes, target, degree)]


WINDOW = window_coefficients(4)


def project(h, gain_row, weight):
    values = h.astype(jnp.float32)
    center = jnp.mean(values, axis=-1, keepdims=True)
    centred = values - center
    spread = jnp.mean(centred * centred, axis=-1, keepdims=True)
    normed = (centred * lax.rsqrt(spread + NORM_EPS) * gain_row).astype(jnp.bfloat16)
    return jnp.dot(normed, weight, preferred_element_type=jnp.float32).astype(jnp.bfloat16)


def tall(block):
    rows, lanes = block.shape
    return jnp.concatenate([block, jnp.zeros((lanes - rows, lanes), block.dtype)], axis=0)


def prepare_tile(t, h, pos, gain_row, weight, charge, k_ref, rhs_ref):
    feats = h.shape[1]
    proj = project(h, gain_row, weight)
    keys = proj[:, feats : 2 * feats]
    k_ref[t] = keys
    rhs_ref[t, :, :feats] = proj[:, 2 * feats :]
    probe = lax.dot_general(
        charge, keys, (((1,), (1,)), ((), ())), preferred_element_type=jnp.float32
    )
    rows = probe * pos
    high = rows.astype(jnp.bfloat16).astype(jnp.float32)
    columns = tall(jnp.concatenate([high, rows - high], axis=0)).T
    rhs_ref[t, :, feats:] = columns.astype(jnp.bfloat16)
    return proj[:, :feats]


def attend_tile(i, own, q, h, pos, noise, scale, slots, k_ref, rhs_ref, pos_ref, s_ref,
                falloff, mixing, out_weight):
    beads, feats = q.shape
    heads = falloff.shape[0]
    head_size = feats // heads
    slot_count = slots.shape[1]
    lane = lax.broadcasted_iota(jnp.int32, (beads, feats), 1) // head_size
    zero = jnp.zeros_like(q)
    stacked = jnp.concatenate([jnp.where(lane == e, q, zero) for e in range(heads)], axis=0)
    columns = tall(pos).T
    where, present = [], []
    for n in range(slot_count):
        slot = slots[i, n]
        present.append((slot >= 0).astype(jnp.float32))
        where.append(jnp.where(slot >= 0, slot, own))
    for first in range(0, slot_count, 2):
        pair = (first, first + 1)
        keys = jnp.concatenate([k_ref[where[n]] for n in pair], axis=0)
        logits = lax.dot_general(
            stacked, keys, (((1,), (1,)), ((), ())), preferred_element_type=jnp.float32
        )
        near = jnp.concatenate([pos_ref[where[n]] for n in pair], axis=1)
        occupied = jnp.concatenate(
            [jnp.full((1, beads), present[n], jnp.float32) for n in pair], axis=1
        )
        squared = None
        for c in range(3):
            offset = columns[:, c : c + 1] - near[c : c + 1, :]
            squared = offset * offset if squared is None else squared + offset * offset
        squared = jnp.minimum(squared, 1.0)
        window = jnp.full_like(squared, WINDOW[0])
        for coefficient in WINDOW[1:]:
            window = window * squared + coefficient
        window = window * (1.0 - squared)
        window = window * window * occupied
        for e in range(heads):
            half = logits[e * beads : (e + 1) * beads]
            act = half + half * jnp.tanh(half)
            score = act * (window * jnp.exp2(squared * (falloff[e] * -LOG2E)))
            s_ref[e * beads : (e + 1) * beads, first * beads : (first + 2) * beads] = score.astype(
                jnp.bfloat16
            )
    rhs = jnp.concatenate([rhs_ref[where[n]] for n in range(slot_count)], axis=0)
    sums = jnp.dot(s_ref[...], rhs, preferred_element_type=jnp.float32)
    message = jnp.zeros((beads, feats), jnp.float32)
    pulls = jnp.zeros((beads, feats), jnp.float32)
    for e in range(heads):
        part = sums[e * beads : (e + 1) * beads]
        message = jnp.where(lane == e, part[:, :feats], message)
        pulls = pulls + mixing[e] * part[:, feats:]
    message = (message * MESSAGE_SCALE).astype(jnp.bfloat16)
    mixed = jnp.dot(message, out_weight, preferred_element_type=jnp.float32)
    updated = (h.astype(jnp.float32) + mixed).astype(jnp.bfloat16)
    turned = pulls.T
    turned = turned[0:8] + turned[8:16]
    force = (pos * turned[3:4] - turned) * FORCE_SCALE
    moved = pos + DURATION_DELTA * force + (JITTER_SIZE * scale) * noise
    return updated, moved, force


def step_kernel(dims, h_ref, pos_ref, noise_ref, slots, heat, falloff, mixing, gain, weight,
                out_weight, charge, h_out, moved_out, force_out, k_ref, rhs_ref, q_ref, s_ref):
    tx, ty = dims
    for t in range((tx + 2) * (ty + 2)):
        q = prepare_tile(t, h_ref[t], pos_ref[t], gain[...], weight[...], charge[...], k_ref, rhs_ref)
        row, col = t // (ty + 2) - 1, t % (ty + 2) - 1
        if 0 <= row < tx and 0 <= col < ty:
            q_ref[row * ty + col] = q * jnp.bfloat16(0.125)

    def body(i, carry):
        own = (i // ty + 1) * (ty + 2) + lax.rem(i, ty) + 1
        updated, moved, force = attend_tile(
            i, own, q_ref[i], h_ref[own], pos_ref[own], noise_ref[i], jnp.sqrt(heat[0:1, 0:1]), slots,
            k_ref, rhs_ref, pos_ref, s_ref, falloff, mixing, out_weight[...])
        h_out[i] = updated
        moved_out[i] = moved
        force_out[i] = force
        return carry

    lax.fori_loop(0, tx * ty, body, 0)


def run_step(h_ext, pos_ext, noise, slots, heat, params, dims):
    gain, weight, out_weight, charge, falloff, mixing = params
    tx, ty = dims
    tiles, ext = tx * ty, (tx + 2) * (ty + 2)
    beads, feats = h_ext.shape[1:]
    heads = falloff.shape[0]
    vmem = pl.BlockSpec(memory_space=pltpu.VMEM)
    smem = pl.BlockSpec(memory_space=pltpu.SMEM)
    return pl.pallas_call(
        functools.partial(step_kernel, dims),
        out_shape=(
            jax.ShapeDtypeStruct((tiles, beads, feats), jnp.bfloat16),
            jax.ShapeDtypeStruct((tiles, 8, beads), jnp.float32),
            jax.ShapeDtypeStruct((tiles, 8, beads), jnp.float32),
        ),
        in_specs=[vmem, vmem, vmem, smem, vmem, smem, smem, vmem, vmem, vmem, vmem],
        out_specs=(vmem, vmem, vmem),
        scratch_shapes=[
            pltpu.VMEM((ext, beads, feats), jnp.bfloat16),
            pltpu.VMEM((ext, beads, 2 * feats), jnp.bfloat16),
            pltpu.VMEM((tiles, beads, feats), jnp.bfloat16),
            pltpu.VMEM((heads * beads, slots.shape[1] * beads), jnp.bfloat16),
        ],
        compiler_params=pltpu.CompilerParams(vmem_limit_bytes=40 * 2**20),
    )(h_ext, pos_ext, noise, slots, heat, falloff, mixing, gain, weight, out_weight, charge)


def with_halo(cells, sides, width):
    for axis, dim in sides:
        count = lax.axis_size(axis)
        ends = count - 1
        head = lax.slice_in_dim(cells, 0, width, axis=dim)
        tail = lax.slice_in_dim(cells, cells.shape[dim] - width, cells.shape[dim], axis=dim)
        cells = jnp.concatenate(
            [
                lax.ppermute(tail, axis, [(i, (i + 1) % count) for i in range(ends)]),
                cells,
                lax.ppermute(head, axis, [((i + 1) % count, i) for i in range(ends)]),
            ],
            axis=dim,
        )
    return cells


def as_rows(coords, fill):
    rows = coords.reshape(3, -1, coords.shape[-1]).transpose(1, 0, 2)
    one = jnp.full_like(rows[:, :1], fill)
    return jnp.concatenate([rows, one, jnp.zeros_like(rows), one * 0], axis=1)


def from_rows(rows, shape):
    return rows[:, :3].transpose(1, 0, 2).reshape(shape)


def per_device(
    particle_descriptors,
    particle_locations_all,
    earlier_jitter,
    later_jitter,
    adjacent_tile_slots,
    thermal_levels,
    heat_slot_of_copy,
    partner_choice,
    normalizer_gain,
    query_lookup_matrix,
    message_output_matrix,
    lookup_charge_map,
    attention_head_falloff,
    attention_head_weight,
):
    feats = normalizer_gain.shape[0]
    params = (
        normalizer_gain.reshape(1, feats),
        query_lookup_matrix,
        message_output_matrix,
        jnp.broadcast_to(lookup_charge_map[None], (8, feats)),
        attention_head_falloff,
        attention_head_weight,
    )
    replicas = thermal_levels.shape[0]
    heat = thermal_levels[heat_slot_of_copy[0]].reshape(1, 1)
    tx, ty = particle_descriptors.shape[1:3]
    slots = adjacent_tile_slots.reshape(tx * ty, -1)

    def step(h, p, noise):
        h_ext = with_halo(h, (("gx", 0), ("gy", 1)), 1)
        p_ext = with_halo(p, (("gx", 1), ("gy", 2)), 1)
        updated, moved, force = run_step(
            h_ext.reshape((-1,) + h.shape[2:]), as_rows(p_ext, 1.0), as_rows(noise, 0.0), slots,
            heat, params, (tx, ty))
        return updated.reshape(h.shape), from_rows(moved, p.shape), from_rows(force, p.shape)

    h, p, _ = step(particle_descriptors[0], particle_locations_all[0], earlier_jitter[0])
    beads = h.shape[2]
    piece = beads // replicas

    def trade(values, flat):
        spread = lax.all_to_all(values.reshape(flat), "rep", split_axis=1, concat_axis=1, tiled=True)
        routed = lax.all_to_all(
            jnp.take(spread, partner_choice, axis=1), "rep", split_axis=1, concat_axis=1, tiled=True
        )
        return routed.reshape(values.shape)

    h = trade(h, (tx * ty, replicas, piece * feats))
    p = trade(p, (3 * tx * ty, replicas, piece))
    h, p, force = step(h, p, later_jitter[0])
    return h[None], p[None], force[None]


def solution(mesh):
    in_specs = (
        P("rep", "gx", "gy", None, None),
        P("rep", None, "gx", "gy", None),
        P("rep", None, "gx", "gy", None),
        P("rep", None, "gx", "gy", None),
        P("gx", "gy", None),
        P(),
        P("rep"),
        P(),
        P(),
        P(),
        P(),
        P(),
        P(),
        P(),
    )
    out_specs = (
        P("rep", "gx", "gy", None, None),
        P("rep", None, "gx", "gy", None),
        P("rep", None, "gx", "gy", None),
    )
    return jax.shard_map(
        per_device, mesh=mesh, in_specs=in_specs, out_specs=out_specs, check_vma=False
    )
```

```python
import functools
import math

import jax
import jax.numpy as jnp
from jax import lax
from jax.experimental import pallas as pl
from jax.experimental.pallas import tpu as pltpu
from jax.sharding import PartitionSpec as P

NORM_EPS = 1e-05
DURATION_DELTA = 0.1
JITTER_SIZE = 0.05
MESSAGE_SCALE = 1.0 / 32.0
FORCE_SCALE = 1.0 / 16.0
LOG2E = math.log2(math.e)


def window_coefficients(degree):
    import numpy as np

    nodes = 0.5 - 0.5 * np.cos(np.pi * (np.arange(64) + 0.5) / 64)
    target = np.cos(0.5 * np.pi * np.sqrt(nodes)) / (1.0 - nodes)
    return [float(c) for c in np.polyfit(nodes, target, degree)]


WINDOW = window_coefficients(4)


def project(h, gain_row, weight):
    values = h.astype(jnp.float32)
    center = jnp.mean(values, axis=-1, keepdims=True)
    centred = values - center
    spread = jnp.mean(centred * centred, axis=-1, keepdims=True)
    normed = (centred * lax.rsqrt(spread + NORM_EPS) * gain_row).astype(jnp.bfloat16)
    return jnp.dot(normed, weight, preferred_element_type=jnp.float32).astype(jnp.bfloat16)


def tall(block):
    rows, lanes = block.shape
    return jnp.concatenate([block, jnp.zeros((lanes - rows, lanes), block.dtype)], axis=0)


def prepare_tile(t, h, pos, gain_row, weight, charge, k_ref, rhs_ref, near_ref):
    feats = h.shape[1]
    proj = project(h, gain_row, weight)
    keys = proj[:, feats : 2 * feats]
    near_ref[t] = pos
    k_ref[t] = keys
    rhs_ref[t, :, :feats] = proj[:, 2 * feats :]
    probe = lax.dot_general(
        charge, keys, (((1,), (1,)), ((), ())), preferred_element_type=jnp.float32
    )
    rows = probe * pos
    high = rows.astype(jnp.bfloat16).astype(jnp.float32)
    columns = tall(jnp.concatenate([high, rows - high], axis=0)).T
    rhs_ref[t, :, feats:] = columns.astype(jnp.bfloat16)
    return proj[:, :feats]


def score_slots(i, group, own, q, pos, slot_of, work, s_ref, falloff):
    k_ref, near_ref = work.k, work.near
    beads, feats = q.shape
    heads = falloff.shape[0]
    lane = lax.broadcasted_iota(jnp.int32, (beads, feats), 1) // (feats // heads)
    zero = jnp.zeros_like(q)
    stacked = jnp.concatenate([jnp.where(lane == e, q, zero) for e in range(heads)], axis=0)
    columns = tall(pos).T
    for part in group:
        where = [jnp.where(slot_of(n) >= 0, slot_of(n), own) for n in part]
        present = [(slot_of(n) >= 0).astype(jnp.float32) for n in part]
        keys = join([k_ref[w] for w in where], 0)
        logits = lax.dot_general(
            stacked, keys, (((1,), (1,)), ((), ())), preferred_element_type=jnp.float32
        )
        near = join([near_ref[w] for w in where], 1)
        occupied = join([jnp.full((1, beads), v, jnp.float32) for v in present], 1)
        squared = None
        for c in range(3):
            offset = columns[:, c : c + 1] - near[c : c + 1, :]
            squared = offset * offset if squared is None else squared + offset * offset
        squared = jnp.minimum(squared, 1.0)
        window = jnp.full_like(squared, WINDOW[0])
        for coefficient in WINDOW[1:]:
            window = window * squared + coefficient
        window = window * (1.0 - squared)
        window = window * window * occupied
        for e in range(heads):
            half = logits[e * beads : (e + 1) * beads]
            act = half + half * jnp.tanh(half)
            score = act * (window * jnp.exp2(squared * (falloff[e] * -LOG2E)))
            s_ref[i, e * beads : (e + 1) * beads, part[0] * beads : (part[-1] + 1) * beads] = (
                score.astype(jnp.bfloat16)
            )


def finish_tile(i, own, h, pos, noise, scale, slot_of, slot_count, work, s_ref, mixing, out_weight):
    beads, feats = h.shape
    heads = mixing.shape[0]
    lane = lax.broadcasted_iota(jnp.int32, (beads, feats), 1) // (feats // heads)
    where = [jnp.where(slot_of(n) >= 0, slot_of(n), own) for n in range(slot_count)]
    rhs = jnp.concatenate([work.rhs[w] for w in where], axis=0)
    sums = jnp.dot(s_ref[i], rhs, preferred_element_type=jnp.float32)
    message = jnp.zeros((beads, feats), jnp.float32)
    pulls = jnp.zeros((beads, feats), jnp.float32)
    for e in range(heads):
        part = sums[e * beads : (e + 1) * beads]
        message = jnp.where(lane == e, part[:, :feats], message)
        pulls = pulls + mixing[e] * part[:, feats:]
    message = (message * MESSAGE_SCALE).astype(jnp.bfloat16)
    mixed = jnp.dot(message, out_weight, preferred_element_type=jnp.float32)
    updated = (h.astype(jnp.float32) + mixed).astype(jnp.bfloat16)
    turned = pulls.T
    turned = turned[0:8] + turned[8:16]
    force = (pos * turned[3:4] - turned) * FORCE_SCALE
    moved = pos + DURATION_DELTA * force + (JITTER_SIZE * scale) * noise
    return updated, moved, force


def join(parts, axis):
    return parts[0] if len(parts) == 1 else jnp.concatenate(parts, axis=axis)


def rows_of(ref, a, b, fill):
    rows = [ref[0, c, a, pl.ds(b, 1), :] for c in range(3)]
    beads = rows[0].shape[1]
    rows.append(jnp.full((1, beads), fill, jnp.float32))
    rows.append(jnp.zeros((4, beads), jnp.float32))
    return jnp.concatenate(rows, axis=0)


class Work:
    def __init__(self, k, rhs, near, q):
        self.k, self.rhs, self.near, self.q = k, rhs, near, q


DIRECTIONS = [(dx, dy) for dx in (-1, 0, 1) for dy in (-1, 0, 1) if (dx, dy) != (0, 0)]


def side(step, size):
    if step == 0:
        return 0, size, 1
    return (size - 1, 1, 0) if step > 0 else (0, 1, size + 1)


def window_kernel(sizes, h_in, p_in, noise1, noise2, slots, levels, heat_slot, partner, gain, weight,
                  out_weight, charge_ref, falloff, mixing, h_out, moved_out, force_out, k_ref,
                  rhs_ref, near_ref, q_ref, s_ref, rim1, rim2, pos1, pos2, mine_h, mine_p, spread_a,
                  spread_b, spread_p, route_h, route_p, trade_h, trade_p, halo_send, halo_recv,
                  swap_send, swap_recv):
    reps, nx, ny = sizes
    _, tx, ty, beads, feats = h_in.shape
    tiles = tx * ty
    ex, ey = tx + 2, ty + 2
    slot_count = slots.shape[2]
    me, gx, gy = lax.axis_index("rep"), lax.axis_index("gx"), lax.axis_index("gy")
    work = Work(k_ref, rhs_ref, near_ref, q_ref)
    scale = jnp.sqrt(jnp.full((1, beads), levels[heat_slot[0]], jnp.float32))
    spread_h = (spread_a, spread_b)
    groups = len(spread_h)
    piece = tiles * beads // groups // reps
    per = mine_p.shape[1]

    def has(dx, dy):
        conds = []
        if dx:
            conds.append(gx < nx - 1 if dx > 0 else gx > 0)
        if dy:
            conds.append(gy < ny - 1 if dy > 0 else gy > 0)
        return conds[0] if len(conds) == 1 else jnp.logical_and(*conds)

    def other(k):
        return (lax.rem(me + k, reps), gx, gy)

    barrier = pltpu.get_barrier_semaphore()
    for k in range(1, reps):
        pl.semaphore_signal(barrier, inc=1, device_id=other(k), device_id_type=pl.DeviceIdType.MESH)
    for dx, dy in DIRECTIONS:
        @pl.when(has(dx, dy))
        def _(dx=dx, dy=dy):
            pl.semaphore_signal(barrier, inc=1, device_id=(me, gx + dx, gy + dy),
                                device_id_type=pl.DeviceIdType.MESH)

    gain_row, weights, out_w = gain[...], weight[...], out_weight[...]
    charge = jnp.broadcast_to(charge_ref[...].astype(jnp.float32), (8, feats)).astype(jnp.bfloat16)

    def prepare(row, col, h, pos):
        q = prepare_tile(row * ey + col, h, pos, gain_row, weights, charge, k_ref, rhs_ref, near_ref)
        if 1 <= row <= tx and 1 <= col <= ty:
            q_ref[(row - 1) * ty + col - 1] = q * jnp.bfloat16(0.125)

    def halo_copies(step, d, h_src, rim, pos):
        dx, dy = DIRECTIONS[d]
        (r0, nr, r1), (c0, nc, c1) = side(dx, tx), side(dy, ty)
        target = (me, gx + dx, gy + dy)
        return [
            pltpu.make_async_remote_copy(
                src_ref=src, dst_ref=dst, send_sem=halo_send.at[step, d, kind],
                recv_sem=halo_recv.at[step, d, kind], device_id=target,
                device_id_type=pl.DeviceIdType.MESH)
            for kind, (src, dst) in enumerate((
                (h_src.at[pl.ds(r0, nr), pl.ds(c0, nc)], rim.at[pl.ds(r1, nr), pl.ds(c1, nc)]),
                (pos.at[pl.ds(r0 + 1, nr), pl.ds(c0 + 1, nc)], pos.at[pl.ds(r1, nr), pl.ds(c1, nc)]),
            ))
        ]

    def slot_reader(i):
        return lambda n: slots[i // ty, lax.rem(i, ty), n]

    def own_of(i):
        return (i // ty + 1) * ey + lax.rem(i, ty) + 1

    def step(number, h_src, rim, pos, noise, finish, after_group):
        for d, (dx, dy) in enumerate(DIRECTIONS):
            @pl.when(has(dx, dy))
            def _(d=d):
                for copy in halo_copies(number, d, h_src, rim, pos):
                    copy.start()

        def self_body(i, carry):
            score_slots(i, ((0,),), own_of(i), q_ref[i], near_ref[own_of(i)], slot_reader(i), work,
                        s_ref, falloff)
            return carry

        lax.fori_loop(0, tiles, self_body, 0)
        for d, (dx, dy) in enumerate(DIRECTIONS):
            @pl.when(has(-dx, -dy))
            def _(d=d, dx=dx, dy=dy):
                for copy in halo_copies(number, d, h_src, rim, pos):
                    copy.wait_recv()
                (_, nr, r1), (_, nc, c1) = side(dx, tx), side(dy, ty)
                for row in range(r1, r1 + nr):
                    for col in range(c1, c1 + nc):
                        prepare(row, col, rim[row, col], pos[row, col])

        rest = [(n, n + 1) if n + 1 < slot_count else (n,) for n in range(1, slot_count, 2)]

        def body(i, carry):
            a, b = i // ty, lax.rem(i, ty)
            here = near_ref[own_of(i)]
            score_slots(i, rest, own_of(i), q_ref[i], here, slot_reader(i), work, s_ref, falloff)
            finish(i, a, b, *finish_tile(
                i, own_of(i), h_src[a, b], here, rows_of(noise, a, b, 0.0), scale, slot_reader(i),
                slot_count, work, s_ref, mixing, out_w))
            return carry

        for g in range(groups):
            lax.fori_loop(g * tiles // groups, (g + 1) * tiles // groups, body, 0)
            after_group(g)
        for d, (dx, dy) in enumerate(DIRECTIONS):
            @pl.when(has(dx, dy))
            def _(d=d):
                for copy in halo_copies(number, d, h_src, rim, pos):
                    copy.wait_send()

    def swap_copy(phase, part, k, src, dst):
        return pltpu.make_async_remote_copy(
            src_ref=src, dst_ref=dst, send_sem=swap_send.at[phase, part, k],
            recv_sem=swap_recv.at[phase, part, k], device_id=other(k),
            device_id_type=pl.DeviceIdType.MESH)

    def first_copy(part, k):
        peer = lax.rem(me + k, reps)
        if part == groups:
            return swap_copy(0, part, k, mine_p.at[peer], spread_p.at[me])
        return swap_copy(0, part, k, mine_h.at[part, peer], spread_h[part].at[me])

    def place(part, owner):
        start = part * (tiles * beads // groups) + owner * piece
        t = start // beads
        return t // ty, lax.rem(t, ty), pl.ds(pl.multiple_of(lax.rem(start, beads), piece), piece)

    def second_copy(part, k):
        if part == groups:
            return swap_copy(1, part, k, route_p.at[k], trade_p.at[me])
        a, b, rows = place(part, me)
        return swap_copy(1, part, k, route_h.at[part, k], trade_h.at[a, b, rows])

    def send_first(part):
        for k in range(1, reps):
            first_copy(part, k).start()
        if part == groups:
            spread_p[me] = mine_p[me]
        else:
            spread_h[part][me] = mine_h[part, me]

    def send_second(part):
        for k in range(1, reps):
            first_copy(part, k).wait_recv()
        for k in range(reps):
            chosen = partner[lax.rem(me + k, reps)]
            if part == groups:
                value = spread_p[chosen]
                if k:
                    route_p[k] = value
                else:
                    trade_p[me] = value
            else:
                value = spread_h[part][chosen]
                if k:
                    route_h[part, k] = value
                else:
                    a, b, rows = place(part, me)
                    trade_h[a, b, rows, :] = value
            if k:
                second_copy(part, k).start()

    def finish_first(i, a, b, updated, moved, force):
        pieces = beads // piece
        for n in range(pieces):
            which = i * pieces + n
            mine_h[which // reps, lax.rem(which, reps)] = updated[n * piece : (n + 1) * piece]
        for c in range(3):
            row = c * tiles + i
            mine_p[row // per, pl.ds(lax.rem(row, per), 1), :] = moved[c : c + 1]

    def after_first(g):
        send_first(g)
        if g:
            send_first(groups)
        if g:
            for part in range(groups + 1):
                send_second(part)

    def finish_second(i, a, b, updated, moved, force):
        h_out[0, a, b] = updated
        for c in range(3):
            moved_out[0, c, a, pl.ds(b, 1), :] = moved[c : c + 1]
            force_out[0, c, a, pl.ds(b, 1), :] = force[c : c + 1]

    for a in range(tx):
        for b in range(ty):
            pos = rows_of(p_in, a, b, 1.0)
            pos1[a + 1, b + 1] = pos
            prepare(a + 1, b + 1, h_in[0, a, b], pos)
    mine_p[...] = jnp.zeros_like(mine_p)

    columns = 1 + jnp.minimum(gx, 1) + jnp.minimum(nx - 1 - gx, 1)
    lines = 1 + jnp.minimum(gy, 1) + jnp.minimum(ny - 1 - gy, 1)
    pl.semaphore_wait(barrier, reps - 2 + columns * lines)

    step(0, h_in.at[0], rim1, pos1, noise1, finish_first, after_first)

    for part in range(groups + 1):
        for k in range(1, reps):
            second_copy(part, k).wait_recv()
    for a in range(tx):
        for b in range(ty):
            rows = []
            for c in range(3):
                row = c * tiles + a * ty + b
                rows.append(trade_p[row // per, row % per : row % per + 1, :])
            rows.append(jnp.full((1, beads), 1.0, jnp.float32))
            rows.append(jnp.zeros((4, beads), jnp.float32))
            pos = jnp.concatenate(rows, axis=0)
            pos2[a + 1, b + 1] = pos
            prepare(a + 1, b + 1, trade_h[a, b], pos)

    step(1, trade_h, rim2, pos2, noise2, finish_second, lambda g: None)
    for part in range(groups + 1):
        for k in range(1, reps):
            first_copy(part, k).wait_send()
            second_copy(part, k).wait_send()


def per_device(
    particle_descriptors,
    particle_locations_all,
    earlier_jitter,
    later_jitter,
    adjacent_tile_slots,
    thermal_levels,
    heat_slot_of_copy,
    partner_choice,
    normalizer_gain,
    query_lookup_matrix,
    message_output_matrix,
    lookup_charge_map,
    attention_head_falloff,
    attention_head_weight,
):
    _, tx, ty, beads, feats = particle_descriptors.shape
    reps, nx, ny = (lax.axis_size(axis) for axis in ("rep", "gx", "gy"))
    tiles, ext = tx * ty, (tx + 2) * (ty + 2)
    heads = attention_head_falloff.shape[0]
    slot_count = adjacent_tile_slots.shape[2]
    groups = 2
    piece = tiles * beads // groups // reps
    per = -(-3 * tiles // reps)
    vmem = pl.BlockSpec(memory_space=pltpu.VMEM)
    smem = pl.BlockSpec(memory_space=pltpu.SMEM)
    bf16, f32 = jnp.bfloat16, jnp.float32
    return pl.pallas_call(
        functools.partial(window_kernel, (reps, nx, ny)),
        out_shape=(
            jax.ShapeDtypeStruct(particle_descriptors.shape, bf16),
            jax.ShapeDtypeStruct(particle_locations_all.shape, f32),
            jax.ShapeDtypeStruct(particle_locations_all.shape, f32),
        ),
        in_specs=[vmem, vmem, vmem, vmem, smem, smem, smem, smem, vmem, vmem, vmem, vmem, smem, smem],
        out_specs=(vmem, vmem, vmem),
        scratch_shapes=[
            pltpu.VMEM((ext, beads, feats), bf16),
            pltpu.VMEM((ext, beads, 2 * feats), bf16),
            pltpu.VMEM((ext, 8, beads), f32),
            pltpu.VMEM((tiles, beads, feats), bf16),
            pltpu.VMEM((tiles, heads * beads, slot_count * beads), bf16),
            pltpu.VMEM((tx + 2, ty + 2, beads, feats), bf16),
            pltpu.VMEM((tx + 2, ty + 2, beads, feats), bf16),
            pltpu.VMEM((tx + 2, ty + 2, 8, beads), f32),
            pltpu.VMEM((tx + 2, ty + 2, 8, beads), f32),
            pltpu.VMEM((groups, reps, piece, feats), bf16),
            pltpu.VMEM((reps, per, beads), f32),
            pltpu.VMEM((reps, piece, feats), bf16),
            pltpu.VMEM((reps, piece, feats), bf16),
            pltpu.VMEM((reps, per, beads), f32),
            pltpu.VMEM((groups, reps, piece, feats), bf16),
            pltpu.VMEM((reps, per, beads), f32),
            pltpu.VMEM((tx, ty, beads, feats), bf16),
            pltpu.VMEM((reps, per, beads), f32),
            pltpu.SemaphoreType.DMA((2, len(DIRECTIONS), 2)),
            pltpu.SemaphoreType.DMA((2, len(DIRECTIONS), 2)),
            pltpu.SemaphoreType.DMA((2, groups + 1, reps)),
            pltpu.SemaphoreType.DMA((2, groups + 1, reps)),
        ],
        compiler_params=pltpu.CompilerParams(
            collective_id=0, has_side_effects=True, vmem_limit_bytes=48 * 2**20
        ),
    )(
        particle_descriptors,
        particle_locations_all,
        earlier_jitter,
        later_jitter,
        adjacent_tile_slots,
        thermal_levels,
        heat_slot_of_copy,
        partner_choice,
        normalizer_gain.reshape(1, feats),
        query_lookup_matrix,
        message_output_matrix,
        lookup_charge_map.reshape(1, feats),
        attention_head_falloff,
        attention_head_weight,
    )


def solution(mesh):
    in_specs = (
        P("rep", "gx", "gy", None, None),
        P("rep", None, "gx", "gy", None),
        P("rep", None, "gx", "gy", None),
        P("rep", None, "gx", "gy", None),
        P("gx", "gy", None),
        P(),
        P("rep"),
        P(),
        P(),
        P(),
        P(),
        P(),
        P(),
        P(),
    )
    out_specs = (
        P("rep", "gx", "gy", None, None),
        P("rep", None, "gx", "gy", None),
        P("rep", None, "gx", "gy", None),
    )
    return jax.shard_map(
        per_device, mesh=mesh, in_specs=in_specs, out_specs=out_specs, check_vma=False
    )
```

```python
import functools
import math

import jax
import jax.numpy as jnp
from jax import lax
from jax.experimental import pallas as pl
from jax.experimental.pallas import tpu as pltpu
from jax.sharding import PartitionSpec as P

NORM_EPS = 1e-05
DURATION_DELTA = 0.1
JITTER_SIZE = 0.05
MESSAGE_SCALE = 1.0 / 32.0
FORCE_SCALE = 1.0 / 16.0
LOG2E = math.log2(math.e)


def window_coefficients(degree):
    import numpy as np

    nodes = 0.5 - 0.5 * np.cos(np.pi * (np.arange(64) + 0.5) / 64)
    target = np.cos(0.5 * np.pi * np.sqrt(nodes)) / (1.0 - nodes)
    return [float(c) for c in np.polyfit(nodes, target, degree)]


WINDOW = window_coefficients(4)
CHUNK = 32


def project(h, gain_row, weight):
    values = h.astype(jnp.float32)
    center = jnp.mean(values, axis=-1, keepdims=True)
    centred = values - center
    spread = jnp.mean(centred * centred, axis=-1, keepdims=True)
    normed = (centred * lax.rsqrt(spread + NORM_EPS) * gain_row).astype(jnp.bfloat16)
    return jnp.dot(normed, weight, preferred_element_type=jnp.float32).astype(jnp.bfloat16)


def tall(block):
    rows, lanes = block.shape
    return jnp.concatenate([block, jnp.zeros((lanes - rows, lanes), block.dtype)], axis=0)


def prepare_features(t, h, gain_row, weight, k_ref, rhs_ref):
    feats = h.shape[1]
    proj = project(h, gain_row, weight)
    k_ref[t] = proj[:, feats : 2 * feats]
    rhs_ref[t, :, :feats] = proj[:, 2 * feats :]
    return proj[:, :feats]


def prepare_force(t, pos, charge, k_ref, rhs_ref, near_ref):
    feats = charge.shape[1]
    near_ref[t] = pos
    probe = lax.dot_general(
        charge, k_ref[t], (((1,), (1,)), ((), ())), preferred_element_type=jnp.float32
    )
    rows = probe * pos
    high = rows.astype(jnp.bfloat16).astype(jnp.float32)
    columns = tall(jnp.concatenate([high, rows - high], axis=0)).T
    rhs_ref[t, :, feats:] = columns.astype(jnp.bfloat16)


def score_slots(i, group, own, q, pos, slot_of, work, s_ref, falloff):
    k_ref, near_ref = work.k, work.near
    beads, feats = q.shape
    heads = falloff.shape[0]
    lane = lax.broadcasted_iota(jnp.int32, (beads, feats), 1) // (feats // heads)
    zero = jnp.zeros_like(q)
    masked = [jnp.where(lane == e, q, zero) for e in range(heads)]
    chunks = range(0, beads, CHUNK)
    stacked = jnp.concatenate([m[r : r + CHUNK] for r in chunks for m in masked], axis=0)
    columns = tall(pos).T
    rates = [falloff[e] * -LOG2E for e in range(heads)]
    for part in group:
        where = [jnp.where(slot_of(n) >= 0, slot_of(n), own) for n in part]
        present = [(slot_of(n) >= 0).astype(jnp.float32) for n in part]
        keys = join([k_ref[w] for w in where], 0)
        logits = lax.dot_general(
            stacked, keys, (((1,), (1,)), ((), ())), preferred_element_type=jnp.float32
        ).astype(jnp.bfloat16)
        near = join([near_ref[w] for w in where], 1)
        occupied = join([jnp.full((1, beads), v, jnp.float32) for v in present], 1)
        for r in chunks:
            squared = None
            for c in range(3):
                offset = columns[r : r + CHUNK, c : c + 1] - near[c : c + 1, :]
                squared = offset * offset if squared is None else squared + offset * offset
            squared = jnp.minimum(squared, 1.0)
            window = jnp.full_like(squared, WINDOW[0])
            for coefficient in WINDOW[1:]:
                window = window * squared + coefficient
            window = window * (1.0 - squared)
            window = (window * window * occupied).astype(jnp.bfloat16)
            for e in range(heads):
                start = r * heads + e * CHUNK
                half = logits[start : start + CHUNK]
                act = half + half * jnp.tanh(half)
                decay = jnp.exp2((squared * rates[e]).astype(jnp.bfloat16))
                s_ref[i, start : start + CHUNK, part[0] * beads : (part[-1] + 1) * beads] = act * (
                    window * decay
                )


def finish_tile(i, own, h, pos, noise, scale, slot_of, slot_count, work, s_ref, mixing, out_weight):
    beads, feats = h.shape
    heads = mixing.shape[0]
    lane = lax.broadcasted_iota(jnp.int32, (CHUNK, feats), 1) // (feats // heads)
    where = [jnp.where(slot_of(n) >= 0, slot_of(n), own) for n in range(slot_count)]
    rhs = jnp.concatenate([work.rhs[w] for w in where], axis=0)
    sums = jnp.dot(s_ref[i], rhs, preferred_element_type=jnp.float32)
    messages, pulls = [], []
    for r in range(0, beads, CHUNK):
        message = jnp.zeros((CHUNK, feats), jnp.float32)
        pull = jnp.zeros((CHUNK, feats), jnp.float32)
        for e in range(heads):
            part = sums[r * heads + e * CHUNK : r * heads + (e + 1) * CHUNK]
            message = jnp.where(lane == e, part[:, :feats], message)
            pull = pull + mixing[e] * part[:, feats:]
        messages.append(message)
        pulls.append(pull)
    message = (jnp.concatenate(messages, axis=0) * MESSAGE_SCALE).astype(jnp.bfloat16)
    pulls = jnp.concatenate(pulls, axis=0)
    mixed = jnp.dot(message, out_weight, preferred_element_type=jnp.float32)
    updated = (h.astype(jnp.float32) + mixed).astype(jnp.bfloat16)
    turned = pulls.T
    turned = turned[0:8] + turned[8:16]
    force = (pos * turned[3:4] - turned) * FORCE_SCALE
    moved = pos + DURATION_DELTA * force + (JITTER_SIZE * scale) * noise
    return updated, moved, force


def join(parts, axis):
    return parts[0] if len(parts) == 1 else jnp.concatenate(parts, axis=axis)


def rows_of(ref, a, b, fill):
    rows = [ref[0, c, a, pl.ds(b, 1), :] for c in range(3)]
    beads = rows[0].shape[1]
    rows.append(jnp.full((1, beads), fill, jnp.float32))
    rows.append(jnp.zeros((4, beads), jnp.float32))
    return jnp.concatenate(rows, axis=0)


OPERANDS = 14


class Work:
    def __init__(self, k, rhs, near, q):
        self.k, self.rhs, self.near, self.q = k, rhs, near, q


DIRECTIONS = [(dx, dy) for dx in (-1, 0, 1) for dy in (-1, 0, 1) if (dx, dy) != (0, 0)]


def side(step, size):
    if step == 0:
        return 0, size, 1
    return (size - 1, 1, 0) if step > 0 else (0, 1, size + 1)


def window_kernel(sizes, *refs):
    operands, refs = refs[:OPERANDS], refs[OPERANDS:]
    outs, held, refs = refs[:3], refs[3 : 3 + OPERANDS], refs[3 + OPERANDS :]
    load_sem, refs = refs[0], refs[1:]
    loads = [
        pltpu.make_async_copy(src, dst, load_sem.at[n])
        for n, (src, dst) in enumerate(zip(operands, held))
    ]
    for load in loads:
        load.start()
    window_body(sizes, loads, *held, *outs, *refs)


def window_body(sizes, loads, h_in, p_in, noise1, noise2, slots, levels, heat_slot, partner, gain,
                  weight, out_weight, charge_ref, falloff, mixing, h_out, moved_out, force_out, k_ref,
                  rhs_ref, near_ref, q_ref, s_ref, rim1, rim2, pos1, pos2, mine_h, mine_p, spread_a,
                  spread_b, spread_p, route_h, route_p, trade_h, trade_p, halo_send, halo_recv,
                  swap_send, swap_recv):
    reps, nx, ny = sizes
    _, tx, ty, beads, feats = h_in.shape
    tiles = tx * ty
    ex, ey = tx + 2, ty + 2
    slot_count = slots.shape[2]
    me, gx, gy = lax.axis_index("rep"), lax.axis_index("gx"), lax.axis_index("gy")
    work = Work(k_ref, rhs_ref, near_ref, q_ref)
    spread_h = (spread_a, spread_b)
    groups = len(spread_h)
    piece = tiles * beads // groups // reps
    per = mine_p.shape[1]

    def has(dx, dy):
        conds = []
        if dx:
            conds.append(gx < nx - 1 if dx > 0 else gx > 0)
        if dy:
            conds.append(gy < ny - 1 if dy > 0 else gy > 0)
        return conds[0] if len(conds) == 1 else jnp.logical_and(*conds)

    def other(k):
        return (lax.rem(me + k, reps), gx, gy)

    barrier = pltpu.get_barrier_semaphore()
    for k in range(1, reps):
        pl.semaphore_signal(barrier, inc=1, device_id=other(k), device_id_type=pl.DeviceIdType.MESH)
    for dx, dy in DIRECTIONS:
        @pl.when(has(dx, dy))
        def _(dx=dx, dy=dy):
            pl.semaphore_signal(barrier, inc=1, device_id=(me, gx + dx, gy + dy),
                                device_id_type=pl.DeviceIdType.MESH)

    for load in loads:
        load.wait()
    scale = jnp.sqrt(jnp.full((1, beads), levels[heat_slot[0]], jnp.float32))
    gain_row, weights, out_w = gain[...], weight[...], out_weight[...]
    charge = jnp.broadcast_to(charge_ref[...].astype(jnp.float32), (8, feats)).astype(jnp.bfloat16)

    def prepare_pos(row, col, pos):
        prepare_force(row * ey + col, pos, charge, k_ref, rhs_ref, near_ref)

    def prepare(row, col, h):
        q = prepare_features(row * ey + col, h, gain_row, weights, k_ref, rhs_ref)
        if 1 <= row <= tx and 1 <= col <= ty:
            q_ref[(row - 1) * ty + col - 1] = q * jnp.bfloat16(0.125)

    def halo_copy(step, d, kind, h_src, rim, pos):
        dx, dy = DIRECTIONS[d]
        (r0, nr, r1), (c0, nc, c1) = side(dx, tx), side(dy, ty)
        target = (me, gx + dx, gy + dy)
        if kind == 0:
            src = h_src.at[pl.ds(r0, nr), pl.ds(c0, nc)]
            dst = rim.at[pl.ds(r1, nr), pl.ds(c1, nc)]
        else:
            src = pos.at[pl.ds(r0 + 1, nr), pl.ds(c0 + 1, nc)]
            dst = pos.at[pl.ds(r1, nr), pl.ds(c1, nc)]
        return pltpu.make_async_remote_copy(
            src_ref=src, dst_ref=dst, send_sem=halo_send.at[step, d, kind],
            recv_sem=halo_recv.at[step, d, kind], device_id=target,
            device_id_type=pl.DeviceIdType.MESH)

    def slot_reader(i):
        return lambda n: slots[i // ty, lax.rem(i, ty), n]

    def own_of(i):
        return (i // ty + 1) * ey + lax.rem(i, ty) + 1

    def start_halo(number, kind, h_src, rim, pos):
        for d, (dx, dy) in enumerate(DIRECTIONS):
            @pl.when(has(dx, dy))
            def _(d=d):
                halo_copy(number, d, kind, h_src, rim, pos).start()

    def step(number, h_src, rim, pos, noise, finish, cuts, after_cut):
        def self_body(i, carry):
            score_slots(i, ((0,),), own_of(i), q_ref[i], near_ref[own_of(i)], slot_reader(i), work,
                        s_ref, falloff)
            return carry

        lax.fori_loop(0, tiles, self_body, 0)
        for d, (dx, dy) in enumerate(DIRECTIONS):
            @pl.when(has(-dx, -dy))
            def _(d=d, dx=dx, dy=dy):
                for kind in range(2):
                    halo_copy(number, d, kind, h_src, rim, pos).wait_recv()
                (_, nr, r1), (_, nc, c1) = side(dx, tx), side(dy, ty)
                for row in range(r1, r1 + nr):
                    for col in range(c1, c1 + nc):
                        prepare(row, col, rim[row, col])
                        prepare_pos(row, col, pos[row, col])

        rest = [(n, n + 1) if n + 1 < slot_count else (n,) for n in range(1, slot_count, 2)]

        def body(i, carry):
            a, b = i // ty, lax.rem(i, ty)
            here = near_ref[own_of(i)]
            score_slots(i, rest, own_of(i), q_ref[i], here, slot_reader(i), work, s_ref, falloff)
            finish(i, a, b, *finish_tile(
                i, own_of(i), h_src[a, b], here, rows_of(noise, a, b, 0.0), scale, slot_reader(i),
                slot_count, work, s_ref, mixing, out_w))
            return carry

        for first, last in zip(cuts[:-1], cuts[1:]):
            lax.fori_loop(first, last, body, 0)
            after_cut(last)
        for d, (dx, dy) in enumerate(DIRECTIONS):
            @pl.when(has(dx, dy))
            def _(d=d):
                for kind in range(2):
                    halo_copy(number, d, kind, h_src, rim, pos).wait_send()

    def swap_copy(phase, part, k, src, dst):
        return pltpu.make_async_remote_copy(
            src_ref=src, dst_ref=dst, send_sem=swap_send.at[phase, part, k],
            recv_sem=swap_recv.at[phase, part, k], device_id=other(k),
            device_id_type=pl.DeviceIdType.MESH)

    def first_copy(part, k):
        peer = lax.rem(me + k, reps)
        if part == groups:
            return swap_copy(0, part, k, mine_p.at[peer], spread_p.at[me])
        return swap_copy(0, part, k, mine_h.at[part, peer], spread_h[part].at[me])

    def place(part, owner):
        start = part * (tiles * beads // groups) + owner * piece
        t = start // beads
        return t // ty, lax.rem(t, ty), pl.ds(pl.multiple_of(lax.rem(start, beads), piece), piece)

    def second_copy(part, k):
        if part == groups:
            return swap_copy(1, part, k, route_p.at[k], trade_p.at[me])
        a, b, rows = place(part, me)
        return swap_copy(1, part, k, route_h.at[part, k], trade_h.at[a, b, rows])

    def send_first(part):
        for k in range(1, reps):
            first_copy(part, k).start()
        if part == groups:
            spread_p[me] = mine_p[me]
        else:
            spread_h[part][me] = mine_h[part, me]

    def send_second(part):
        for k in range(1, reps):
            first_copy(part, k).wait_recv()
        for k in range(reps):
            chosen = partner[lax.rem(me + k, reps)]
            if part == groups:
                value = spread_p[chosen]
                if k:
                    route_p[k] = value
                else:
                    trade_p[me] = value
            else:
                value = spread_h[part][chosen]
                if k:
                    route_h[part, k] = value
                else:
                    a, b, rows = place(part, me)
                    trade_h[a, b, rows, :] = value
            if k:
                second_copy(part, k).start()

    def finish_first(i, a, b, updated, moved, force):
        pieces = beads // piece
        for n in range(pieces):
            which = i * pieces + n
            mine_h[which // reps, lax.rem(which, reps)] = updated[n * piece : (n + 1) * piece]
        for c in range(3):
            row = c * tiles + i
            mine_p[row // per, pl.ds(lax.rem(row, per), 1), :] = moved[c : c + 1]

    def after_first(done):
        if done == tiles // groups:
            send_first(0)
        elif done < tiles:
            send_second(0)
        else:
            send_first(groups)
            send_first(1)
            send_second(groups)
            send_second(1)

    def finish_second(i, a, b, updated, moved, force):
        h_out[0, a, b] = updated
        for c in range(3):
            moved_out[0, c, a, pl.ds(b, 1), :] = moved[c : c + 1]
            force_out[0, c, a, pl.ds(b, 1), :] = force[c : c + 1]

    grid = [(a, b) for a in range(tx) for b in range(ty)]
    half_tiles = tiles // groups
    for a, b in grid:
        pos1[a + 1, b + 1] = rows_of(p_in, a, b, 1.0)
    for a, b in grid[:half_tiles]:
        prepare(a + 1, b + 1, h_in[0, a, b])
    mine_p[...] = jnp.zeros_like(mine_p)

    columns = 1 + jnp.minimum(gx, 1) + jnp.minimum(nx - 1 - gx, 1)
    lines = 1 + jnp.minimum(gy, 1) + jnp.minimum(ny - 1 - gy, 1)
    pl.semaphore_wait(barrier, reps - 2 + columns * lines)

    for kind in range(2):
        start_halo(0, kind, h_in.at[0], rim1, pos1)
    for a, b in grid[half_tiles:]:
        prepare(a + 1, b + 1, h_in[0, a, b])
    for a, b in grid:
        prepare_pos(a + 1, b + 1, rows_of(p_in, a, b, 1.0))
    cuts = (0, half_tiles, tiles - 1, tiles)
    step(0, h_in.at[0], rim1, pos1, noise1, finish_first, cuts, after_first)

    def arrive(part):
        for k in range(1, reps):
            second_copy(part, k).wait_recv()

    arrive(0)
    for a, b in grid[:half_tiles]:
        prepare(a + 1, b + 1, trade_h[a, b])
    arrive(groups)
    for a, b in grid:
        rows = []
        for c in range(3):
            row = c * tiles + a * ty + b
            rows.append(trade_p[row // per, row % per : row % per + 1, :])
        rows.append(jnp.full((1, beads), 1.0, jnp.float32))
        rows.append(jnp.zeros((4, beads), jnp.float32))
        pos2[a + 1, b + 1] = jnp.concatenate(rows, axis=0)
    start_halo(1, 1, trade_h, rim2, pos2)
    arrive(1)
    start_halo(1, 0, trade_h, rim2, pos2)
    for a, b in grid[half_tiles:]:
        prepare(a + 1, b + 1, trade_h[a, b])
    for a, b in grid:
        prepare_pos(a + 1, b + 1, pos2[a + 1, b + 1])
    step(1, trade_h, rim2, pos2, noise2, finish_second, (0, tiles), lambda done: None)
    for part in range(groups + 1):
        for k in range(1, reps):
            first_copy(part, k).wait_send()
            second_copy(part, k).wait_send()


def per_device(
    particle_descriptors,
    particle_locations_all,
    earlier_jitter,
    later_jitter,
    adjacent_tile_slots,
    thermal_levels,
    heat_slot_of_copy,
    partner_choice,
    normalizer_gain,
    query_lookup_matrix,
    message_output_matrix,
    lookup_charge_map,
    attention_head_falloff,
    attention_head_weight,
):
    _, tx, ty, beads, feats = particle_descriptors.shape
    reps, nx, ny = (lax.axis_size(axis) for axis in ("rep", "gx", "gy"))
    tiles, ext = tx * ty, (tx + 2) * (ty + 2)
    heads = attention_head_falloff.shape[0]
    slot_count = adjacent_tile_slots.shape[2]
    groups = 2
    piece = tiles * beads // groups // reps
    per = -(-3 * tiles // reps)
    vmem = pl.BlockSpec(memory_space=pltpu.VMEM)
    bf16, f32 = jnp.bfloat16, jnp.float32
    operands = (
        particle_descriptors,
        particle_locations_all,
        earlier_jitter,
        later_jitter,
        adjacent_tile_slots,
        thermal_levels,
        heat_slot_of_copy,
        partner_choice,
        normalizer_gain.reshape(1, feats),
        query_lookup_matrix,
        message_output_matrix,
        lookup_charge_map.reshape(1, feats),
        attention_head_falloff,
        attention_head_weight,
    )
    return pl.pallas_call(
        functools.partial(window_kernel, (reps, nx, ny)),
        out_shape=(
            jax.ShapeDtypeStruct(particle_descriptors.shape, bf16),
            jax.ShapeDtypeStruct(particle_locations_all.shape, f32),
            jax.ShapeDtypeStruct(particle_locations_all.shape, f32),
        ),
        in_specs=[pl.BlockSpec(memory_space=pltpu.HBM)] * OPERANDS,
        out_specs=(vmem, vmem, vmem),
        scratch_shapes=[
            (pltpu.SMEM if n in (4, 5, 6, 7, 12, 13) else pltpu.VMEM)(x.shape, x.dtype)
            for n, x in enumerate(operands)
        ]
        + [
            pltpu.SemaphoreType.DMA((OPERANDS,)),
            pltpu.VMEM((ext, beads, feats), bf16),
            pltpu.VMEM((ext, beads, 2 * feats), bf16),
            pltpu.VMEM((ext, 8, beads), f32),
            pltpu.VMEM((tiles, beads, feats), bf16),
            pltpu.VMEM((tiles, heads * beads, slot_count * beads), bf16),
            pltpu.VMEM((tx + 2, ty + 2, beads, feats), bf16),
            pltpu.VMEM((tx + 2, ty + 2, beads, feats), bf16),
            pltpu.VMEM((tx + 2, ty + 2, 8, beads), f32),
            pltpu.VMEM((tx + 2, ty + 2, 8, beads), f32),
            pltpu.VMEM((groups, reps, piece, feats), bf16),
            pltpu.VMEM((reps, per, beads), f32),
            pltpu.VMEM((reps, piece, feats), bf16),
            pltpu.VMEM((reps, piece, feats), bf16),
            pltpu.VMEM((reps, per, beads), f32),
            pltpu.VMEM((groups, reps, piece, feats), bf16),
            pltpu.VMEM((reps, per, beads), f32),
            pltpu.VMEM((tx, ty, beads, feats), bf16),
            pltpu.VMEM((reps, per, beads), f32),
            pltpu.SemaphoreType.DMA((2, len(DIRECTIONS), 2)),
            pltpu.SemaphoreType.DMA((2, len(DIRECTIONS), 2)),
            pltpu.SemaphoreType.DMA((2, groups + 1, reps)),
            pltpu.SemaphoreType.DMA((2, groups + 1, reps)),
        ],
        compiler_params=pltpu.CompilerParams(
            collective_id=0, has_side_effects=True, vmem_limit_bytes=60 * 2**20
        ),
    )(*operands)


def solution(mesh):
    in_specs = (
        P("rep", "gx", "gy", None, None),
        P("rep", None, "gx", "gy", None),
        P("rep", None, "gx", "gy", None),
        P("rep", None, "gx", "gy", None),
        P("gx", "gy", None),
        P(),
        P("rep"),
        P(),
        P(),
        P(),
        P(),
        P(),
        P(),
        P(),
    )
    out_specs = (
        P("rep", "gx", "gy", None, None),
        P("rep", None, "gx", "gy", None),
        P("rep", None, "gx", "gy", None),
    )
    return jax.shard_map(
        per_device, mesh=mesh, in_specs=in_specs, out_specs=out_specs, check_vma=False
    )
```

```python
import functools
import math

import jax
import jax.numpy as jnp
from jax import lax
from jax.experimental import pallas as pl
from jax.experimental.pallas import tpu as pltpu
from jax.sharding import PartitionSpec as P

NORM_EPS = 1e-05
DURATION_DELTA = 0.1
JITTER_SIZE = 0.05
MESSAGE_SCALE = 1.0 / 32.0
FORCE_SCALE = 1.0 / 16.0
LOG2E = math.log2(math.e)


def window_coefficients(degree):
    import numpy as np

    nodes = 0.5 - 0.5 * np.cos(np.pi * (np.arange(64) + 0.5) / 64)
    target = np.cos(0.5 * np.pi * np.sqrt(nodes)) / (1.0 - nodes)
    return [float(c) for c in np.polyfit(nodes, target, degree)]


WINDOW = window_coefficients(4)
CHUNK = 32


def project(h, gain_row, weight):
    values = h.astype(jnp.float32)
    center = jnp.mean(values, axis=-1, keepdims=True)
    centred = values - center
    spread = jnp.mean(centred * centred, axis=-1, keepdims=True)
    normed = (centred * lax.rsqrt(spread + NORM_EPS) * gain_row).astype(jnp.bfloat16)
    return jnp.dot(normed, weight, preferred_element_type=jnp.float32).astype(jnp.bfloat16)


def tall(block):
    rows, lanes = block.shape
    return jnp.concatenate([block, jnp.zeros((lanes - rows, lanes), block.dtype)], axis=0)


def prepare_features(t, h, gain_row, weight, k_ref, rhs_ref):
    feats = h.shape[1]
    proj = project(h, gain_row, weight)
    k_ref[t] = proj[:, feats : 2 * feats]
    rhs_ref[t, :, :feats] = proj[:, 2 * feats :]
    return proj[:, :feats]


def prepare_force(t, pos, charge, k_ref, rhs_ref, near_ref):
    feats = charge.shape[1]
    near_ref[t] = pos
    probe = lax.dot_general(
        charge, k_ref[t], (((1,), (1,)), ((), ())), preferred_element_type=jnp.float32
    )
    rows = probe * pos
    high = rows.astype(jnp.bfloat16).astype(jnp.float32)
    columns = tall(jnp.concatenate([high, rows - high], axis=0)).T
    rhs_ref[t, :, feats:] = columns.astype(jnp.bfloat16)


def score_slots(i, group, own, q, pos, slot_of, work, s_ref, falloff):
    k_ref, near_ref = work.k, work.near
    beads, feats = q.shape
    heads = falloff.shape[0]
    lane = lax.broadcasted_iota(jnp.int32, (beads, feats), 1) // (feats // heads)
    zero = jnp.zeros_like(q)
    masked = [jnp.where(lane == e, q, zero) for e in range(heads)]
    chunks = range(0, beads, CHUNK)
    stacked = jnp.concatenate([m[r : r + CHUNK] for r in chunks for m in masked], axis=0)
    columns = tall(pos).T
    rates = [falloff[e] * -LOG2E for e in range(heads)]
    for part in group:
        where = [jnp.where(slot_of(n) >= 0, slot_of(n), own) for n in part]
        present = [(slot_of(n) >= 0).astype(jnp.float32) for n in part]
        keys = join([k_ref[w] for w in where], 0)
        logits = lax.dot_general(
            stacked, keys, (((1,), (1,)), ((), ())), preferred_element_type=jnp.float32
        ).astype(jnp.bfloat16)
        near = join([near_ref[w] for w in where], 1)
        occupied = join([jnp.full((1, beads), v, jnp.float32) for v in present], 1)
        for r in chunks:
            squared = None
            for c in range(3):
                offset = columns[r : r + CHUNK, c : c + 1] - near[c : c + 1, :]
                squared = offset * offset if squared is None else squared + offset * offset
            squared = jnp.minimum(squared, 1.0)
            window = jnp.full_like(squared, WINDOW[0])
            for coefficient in WINDOW[1:]:
                window = window * squared + coefficient
            window = window * (1.0 - squared)
            window = window * window * occupied
            for e in range(heads):
                start = r * heads + e * CHUNK
                half = logits[start : start + CHUNK]
                act = half + half * jnp.tanh(half)
                decay = window * jnp.exp2(squared * rates[e])
                s_ref[i, start : start + CHUNK, part[0] * beads : (part[-1] + 1) * beads] = (
                    act * decay.astype(jnp.bfloat16)
                )


def finish_tile(i, own, h, pos, noise, scale, slot_of, slot_count, work, s_ref, mixing, out_weight):
    beads, feats = h.shape
    heads = mixing.shape[0]
    lane = lax.broadcasted_iota(jnp.int32, (CHUNK, feats), 1) // (feats // heads)
    where = [jnp.where(slot_of(n) >= 0, slot_of(n), own) for n in range(slot_count)]
    rhs = jnp.concatenate([work.rhs[w] for w in where], axis=0)
    sums = jnp.dot(s_ref[i], rhs, preferred_element_type=jnp.float32)
    messages, pulls = [], []
    for r in range(0, beads, CHUNK):
        message = jnp.zeros((CHUNK, feats), jnp.float32)
        pull = jnp.zeros((CHUNK, feats), jnp.float32)
        for e in range(heads):
            part = sums[r * heads + e * CHUNK : r * heads + (e + 1) * CHUNK]
            message = jnp.where(lane == e, part[:, :feats], message)
            pull = pull + mixing[e] * part[:, feats:]
        messages.append(message)
        pulls.append(pull)
    message = (jnp.concatenate(messages, axis=0) * MESSAGE_SCALE).astype(jnp.bfloat16)
    pulls = jnp.concatenate(pulls, axis=0)
    mixed = jnp.dot(message, out_weight, preferred_element_type=jnp.float32)
    updated = (h.astype(jnp.float32) + mixed).astype(jnp.bfloat16)
    turned = pulls.T
    turned = turned[0:8] + turned[8:16]
    force = (pos * turned[3:4] - turned) * FORCE_SCALE
    moved = pos + DURATION_DELTA * force + (JITTER_SIZE * scale) * noise
    return updated, moved, force


def join(parts, axis):
    return parts[0] if len(parts) == 1 else jnp.concatenate(parts, axis=axis)


def rows_of(ref, a, b, fill):
    rows = [ref[c, a, pl.ds(b, 1), :] for c in range(3)]
    beads = rows[0].shape[1]
    rows.append(jnp.full((1, beads), fill, jnp.float32))
    rows.append(jnp.zeros((4, beads), jnp.float32))
    return jnp.concatenate(rows, axis=0)


OPERANDS = 14


class Work:
    def __init__(self, k, rhs, near, q):
        self.k, self.rhs, self.near, self.q = k, rhs, near, q


DIRECTIONS = [(dx, dy) for dx in (-1, 0, 1) for dy in (-1, 0, 1) if (dx, dy) != (0, 0)]


def side(step, size):
    if step == 0:
        return 0, size, 1
    return (size - 1, 1, 0) if step > 0 else (0, 1, size + 1)


def window_kernel(sizes, *refs):
    operands, refs = refs[:OPERANDS], refs[OPERANDS:]
    outs, held, refs = refs[:3], refs[3 : OPERANDS + 2], refs[OPERANDS + 2 :]
    load_sem, refs = refs[0], refs[1:]
    feats_of, noise = held[0], held[2]
    places = [feats_of.at[pl.ds(0, 1)], held[1], noise.at[pl.ds(0, 1)], noise.at[pl.ds(1, 1)]]
    loads = [
        pltpu.make_async_copy(src, dst, load_sem.at[n])
        for n, (src, dst) in enumerate(zip(operands, places + list(held[3:])))
    ]
    for load in loads:
        load.start()
    window_body(sizes, loads, *held, *outs, *refs)


def window_body(sizes, loads, h_both, p_in, noise_both, slots, levels, heat_slot, partner, gain,
                  weight, out_weight, charge_ref, falloff, mixing, h_out, moved_out, force_out, k_ref,
                  rhs_ref, near_ref, q_ref, s_ref, rim_both, pos_both, mine_h, mine_p, spread_a,
                  spread_b, spread_p, route_h, route_p, trade_p, halo_send, halo_recv,
                  swap_send, swap_recv):
    reps, nx, ny = sizes
    _, tx, ty, beads, feats = h_both.shape
    trade_h = h_both.at[1]
    tiles = tx * ty
    ex, ey = tx + 2, ty + 2
    slot_count = slots.shape[2]
    me, gx, gy = lax.axis_index("rep"), lax.axis_index("gx"), lax.axis_index("gy")
    work = Work(k_ref, rhs_ref, near_ref, q_ref)
    spread_h = (spread_a, spread_b)
    groups = len(spread_h)
    piece = tiles * beads // groups // reps
    per = mine_p.shape[1]

    def has(dx, dy):
        conds = []
        if dx:
            conds.append(gx < nx - 1 if dx > 0 else gx > 0)
        if dy:
            conds.append(gy < ny - 1 if dy > 0 else gy > 0)
        return conds[0] if len(conds) == 1 else jnp.logical_and(*conds)

    def other(k):
        return (lax.rem(me + k, reps), gx, gy)

    barrier = pltpu.get_barrier_semaphore()
    for k in range(1, reps):
        pl.semaphore_signal(barrier, inc=1, device_id=other(k), device_id_type=pl.DeviceIdType.MESH)
    for dx, dy in DIRECTIONS:
        @pl.when(has(dx, dy))
        def _(dx=dx, dy=dy):
            pl.semaphore_signal(barrier, inc=1, device_id=(me, gx + dx, gy + dy),
                                device_id_type=pl.DeviceIdType.MESH)

    for load in loads:
        load.wait()
    scale = jnp.sqrt(jnp.full((1, beads), levels[heat_slot[0]], jnp.float32))
    gain_row, weights, out_w = gain[...], weight[...], out_weight[...]
    charge = jnp.broadcast_to(charge_ref[...].astype(jnp.float32), (8, feats)).astype(jnp.bfloat16)

    def prepare(row, col, h, pos, inner):
        t = row * ey + col
        q = prepare_features(t, h, gain_row, weights, k_ref, rhs_ref)
        if inner:
            q_ref[(row - 1) * ty + col - 1] = q * jnp.bfloat16(0.125)
        prepare_force(t, pos, charge, k_ref, rhs_ref, near_ref)

    def halo_copy(step, d, kind):
        dx, dy = DIRECTIONS[d]
        (r0, nr, r1), (c0, nc, c1) = side(dx, tx), side(dy, ty)
        target = (me, gx + dx, gy + dy)
        h_src, rim, pos = h_both.at[step], rim_both.at[step], pos_both.at[step]
        if kind == 0:
            src = h_src.at[pl.ds(r0, nr), pl.ds(c0, nc)]
            dst = rim.at[pl.ds(r1, nr), pl.ds(c1, nc)]
        else:
            src = pos.at[pl.ds(r0 + 1, nr), pl.ds(c0 + 1, nc)]
            dst = pos.at[pl.ds(r1, nr), pl.ds(c1, nc)]
        return pltpu.make_async_remote_copy(
            src_ref=src, dst_ref=dst, send_sem=halo_send.at[step, d, kind],
            recv_sem=halo_recv.at[step, d, kind], device_id=target,
            device_id_type=pl.DeviceIdType.MESH)

    def slot_reader(i):
        return lambda n: slots[i // ty, lax.rem(i, ty), n]

    def own_of(i):
        return (i // ty + 1) * ey + lax.rem(i, ty) + 1

    def each_direction(act, sign):
        for d, (dx, dy) in enumerate(DIRECTIONS):
            @pl.when(has(sign * dx, sign * dy))
            def _(d=d):
                for kind in range(2):
                    act(d, kind)

    def step(number):
        each_direction(lambda d, kind: halo_copy(number, d, kind).start(), 1)

        def inner_body(a, carry):
            for b in range(ty):
                prepare(a + 1, b + 1, h_both[number, a, b], pos_both[number, a + 1, b + 1], True)
            return carry

        lax.fori_loop(0, tx, inner_body, 0)

        def self_body(i, carry):
            score_slots(i, ((0,),), own_of(i), q_ref[i], near_ref[own_of(i)], slot_reader(i), work,
                        s_ref, falloff)
            return carry

        lax.fori_loop(0, tiles, self_body, 0)
        each_direction(lambda d, kind: halo_copy(number, d, kind).wait_recv(), -1)

        def rim_body(t, carry):
            row, col = t // ey, lax.rem(t, ey)
            inside = (row >= 1) & (row <= tx) & (col >= 1) & (col <= ty)
            near_x = ((row >= 1) | (gx > 0)) & ((row <= tx) | (gx < nx - 1))
            near_y = ((col >= 1) | (gy > 0)) & ((col <= ty) | (gy < ny - 1))

            @pl.when(near_x & near_y & jnp.logical_not(inside))
            def _():
                prepare(row, col, rim_both[number, row, col], pos_both[number, row, col], False)

            return carry

        lax.fori_loop(0, ex * ey, rim_body, 0)
        rest = [(n, n + 1) if n + 1 < slot_count else (n,) for n in range(1, slot_count, 2)]

        def body(i, carry):
            a, b = i // ty, lax.rem(i, ty)
            here = near_ref[own_of(i)]
            score_slots(i, rest, own_of(i), q_ref[i], here, slot_reader(i), work, s_ref, falloff)
            updated, moved, force = finish_tile(
                i, own_of(i), h_both[number, a, b], here, rows_of(noise_both.at[number], a, b, 0.0),
                scale, slot_reader(i), slot_count, work, s_ref, mixing, out_w)

            @pl.when(number == 0)
            def _():
                finish_first(i, a, b, updated, moved, force)

            @pl.when(number == 1)
            def _():
                finish_second(i, a, b, updated, moved, force)

            for done in (tiles // groups, tiles - 1):
                @pl.when((number == 0) & (i == done - 1))
                def _(done=done):
                    after_first(done)

            return carry

        lax.fori_loop(0, tiles, body, 0)

        @pl.when(number == 0)
        def _():
            after_first(tiles)
            exchange_end()

        each_direction(lambda d, kind: halo_copy(number, d, kind).wait_send(), 1)

    def swap_copy(phase, part, k, src, dst):
        return pltpu.make_async_remote_copy(
            src_ref=src, dst_ref=dst, send_sem=swap_send.at[phase, part, k],
            recv_sem=swap_recv.at[phase, part, k], device_id=other(k),
            device_id_type=pl.DeviceIdType.MESH)

    def first_copy(part, k):
        peer = lax.rem(me + k, reps)
        if part == groups:
            return swap_copy(0, part, k, mine_p.at[peer], spread_p.at[me])
        return swap_copy(0, part, k, mine_h.at[part, peer], spread_h[part].at[me])

    def place(part, owner):
        start = part * (tiles * beads // groups) + owner * piece
        t = start // beads
        return t // ty, lax.rem(t, ty), pl.ds(pl.multiple_of(lax.rem(start, beads), piece), piece)

    def second_copy(part, k):
        if part == groups:
            return swap_copy(1, part, k, route_p.at[k], trade_p.at[me])
        a, b, rows = place(part, me)
        return swap_copy(1, part, k, route_h.at[part, k], trade_h.at[a, b, rows])

    def send_first(part):
        for k in range(1, reps):
            first_copy(part, k).start()
        if part == groups:
            spread_p[me] = mine_p[me]
        else:
            spread_h[part][me] = mine_h[part, me]

    def send_second(part):
        for k in range(1, reps):
            first_copy(part, k).wait_recv()
        for k in range(reps):
            chosen = partner[lax.rem(me + k, reps)]
            if part == groups:
                value = spread_p[chosen]
                if k:
                    route_p[k] = value
                else:
                    trade_p[me] = value
            else:
                value = spread_h[part][chosen]
                if k:
                    route_h[part, k] = value
                else:
                    a, b, rows = place(part, me)
                    trade_h[a, b, rows, :] = value
            if k:
                second_copy(part, k).start()

    def finish_first(i, a, b, updated, moved, force):
        pieces = beads // piece
        for n in range(pieces):
            which = i * pieces + n
            mine_h[which // reps, lax.rem(which, reps)] = updated[n * piece : (n + 1) * piece]
        for c in range(3):
            row = c * tiles + i
            mine_p[row // per, pl.ds(lax.rem(row, per), 1), :] = moved[c : c + 1]

    def after_first(done):
        if done == tiles // groups:
            send_first(0)
        elif done < tiles:
            send_second(0)
        else:
            send_first(groups)
            send_first(1)
            send_second(groups)
            send_second(1)

    def finish_second(i, a, b, updated, moved, force):
        h_out[0, a, b] = updated
        for c in range(3):
            moved_out[0, c, a, pl.ds(b, 1), :] = moved[c : c + 1]
            force_out[0, c, a, pl.ds(b, 1), :] = force[c : c + 1]

    def place_pos(number, a, b, rows):
        rows = rows + [jnp.full((1, beads), 1.0, jnp.float32), jnp.zeros((4, beads), jnp.float32)]
        pos_both[number, a + 1, b + 1] = jnp.concatenate(rows, axis=0)

    def exchange_end():
        for part in range(groups + 1):
            for k in range(1, reps):
                second_copy(part, k).wait_recv()
        for a in range(tx):
            for b in range(ty):
                at = [c * tiles + a * ty + b for c in range(3)]
                place_pos(1, a, b, [trade_p[r // per, r % per : r % per + 1, :] for r in at])

    for a in range(tx):
        for b in range(ty):
            place_pos(0, a, b, [p_in[0, c, a, b : b + 1, :] for c in range(3)])
    mine_p[...] = jnp.zeros_like(mine_p)
    columns = 1 + jnp.minimum(gx, 1) + jnp.minimum(nx - 1 - gx, 1)
    lines = 1 + jnp.minimum(gy, 1) + jnp.minimum(ny - 1 - gy, 1)
    pl.semaphore_wait(barrier, reps - 2 + columns * lines)

    def steps(number, carry):
        step(number)
        return carry

    lax.fori_loop(0, 2, steps, 0)
    for part in range(groups + 1):
        for k in range(1, reps):
            first_copy(part, k).wait_send()
            second_copy(part, k).wait_send()


def per_device(
    particle_descriptors,
    particle_locations_all,
    earlier_jitter,
    later_jitter,
    adjacent_tile_slots,
    thermal_levels,
    heat_slot_of_copy,
    partner_choice,
    normalizer_gain,
    query_lookup_matrix,
    message_output_matrix,
    lookup_charge_map,
    attention_head_falloff,
    attention_head_weight,
):
    _, tx, ty, beads, feats = particle_descriptors.shape
    reps, nx, ny = (lax.axis_size(axis) for axis in ("rep", "gx", "gy"))
    tiles, ext = tx * ty, (tx + 2) * (ty + 2)
    heads = attention_head_falloff.shape[0]
    slot_count = adjacent_tile_slots.shape[2]
    groups = 2
    piece = tiles * beads // groups // reps
    per = -(-3 * tiles // reps)
    vmem = pl.BlockSpec(memory_space=pltpu.VMEM)
    bf16, f32 = jnp.bfloat16, jnp.float32
    operands = (
        particle_descriptors,
        particle_locations_all,
        earlier_jitter,
        later_jitter,
        adjacent_tile_slots,
        thermal_levels,
        heat_slot_of_copy,
        partner_choice,
        normalizer_gain.reshape(1, feats),
        query_lookup_matrix,
        message_output_matrix,
        lookup_charge_map.reshape(1, feats),
        attention_head_falloff,
        attention_head_weight,
    )
    return pl.pallas_call(
        functools.partial(window_kernel, (reps, nx, ny)),
        out_shape=(
            jax.ShapeDtypeStruct(particle_descriptors.shape, bf16),
            jax.ShapeDtypeStruct(particle_locations_all.shape, f32),
            jax.ShapeDtypeStruct(particle_locations_all.shape, f32),
        ),
        in_specs=[pl.BlockSpec(memory_space=pltpu.HBM)] * OPERANDS,
        out_specs=(vmem, vmem, vmem),
        scratch_shapes=[
            pltpu.VMEM((2, tx, ty, beads, feats), bf16),
            pltpu.VMEM(particle_locations_all.shape, f32),
            pltpu.VMEM((2, 3, tx, ty, beads), f32),
        ]
        + [
            (pltpu.SMEM if n in (4, 5, 6, 7, 12, 13) else pltpu.VMEM)(x.shape, x.dtype)
            for n, x in enumerate(operands)
            if n >= 4
        ]
        + [
            pltpu.SemaphoreType.DMA((OPERANDS,)),
            pltpu.VMEM((ext, beads, feats), bf16),
            pltpu.VMEM((ext, beads, 2 * feats), bf16),
            pltpu.VMEM((ext, 8, beads), f32),
            pltpu.VMEM((tiles, beads, feats), bf16),
            pltpu.VMEM((tiles, heads * beads, slot_count * beads), bf16),
            pltpu.VMEM((2, tx + 2, ty + 2, beads, feats), bf16),
            pltpu.VMEM((2, tx + 2, ty + 2, 8, beads), f32),
            pltpu.VMEM((groups, reps, piece, feats), bf16),
            pltpu.VMEM((reps, per, beads), f32),
            pltpu.VMEM((reps, piece, feats), bf16),
            pltpu.VMEM((reps, piece, feats), bf16),
            pltpu.VMEM((reps, per, beads), f32),
            pltpu.VMEM((groups, reps, piece, feats), bf16),
            pltpu.VMEM((reps, per, beads), f32),
            pltpu.VMEM((reps, per, beads), f32),
            pltpu.SemaphoreType.DMA((2, len(DIRECTIONS), 2)),
            pltpu.SemaphoreType.DMA((2, len(DIRECTIONS), 2)),
            pltpu.SemaphoreType.DMA((2, groups + 1, reps)),
            pltpu.SemaphoreType.DMA((2, groups + 1, reps)),
        ],
        compiler_params=pltpu.CompilerParams(
            collective_id=0, has_side_effects=True, vmem_limit_bytes=60 * 2**20
        ),
    )(*operands)


def solution(mesh):
    in_specs = (
        P("rep", "gx", "gy", None, None),
        P("rep", None, "gx", "gy", None),
        P("rep", None, "gx", "gy", None),
        P("rep", None, "gx", "gy", None),
        P("gx", "gy", None),
        P(),
        P("rep"),
        P(),
        P(),
        P(),
        P(),
        P(),
        P(),
        P(),
    )
    out_specs = (
        P("rep", "gx", "gy", None, None),
        P("rep", None, "gx", "gy", None),
        P("rep", None, "gx", "gy", None),
    )
    return jax.shard_map(
        per_device, mesh=mesh, in_specs=in_specs, out_specs=out_specs, check_vma=False
    )
```

```python
import functools
import math

import jax
import jax.numpy as jnp
from jax import lax
from jax.experimental import pallas as pl
from jax.experimental.pallas import tpu as pltpu
from jax.sharding import PartitionSpec as P

NORM_EPS = 1e-05
DURATION_DELTA = 0.1
JITTER_SIZE = 0.05
MESSAGE_SCALE = 1.0 / 32.0
FORCE_SCALE = 1.0 / 16.0
LOG2E = math.log2(math.e)


def window_coefficients(degree):
    import numpy as np

    nodes = 0.5 - 0.5 * np.cos(np.pi * (np.arange(64) + 0.5) / 64)
    target = np.cos(0.5 * np.pi * np.sqrt(nodes)) / (1.0 - nodes)
    return [float(c) for c in np.polyfit(nodes, target, degree)]


WINDOW = window_coefficients(4)
CHUNK = 32


def project(h, gain_row, weight):
    values = h.astype(jnp.float32)
    center = jnp.mean(values, axis=-1, keepdims=True)
    centred = values - center
    spread = jnp.mean(centred * centred, axis=-1, keepdims=True)
    normed = (centred * lax.rsqrt(spread + NORM_EPS) * gain_row).astype(jnp.bfloat16)
    return jnp.dot(normed, weight, preferred_element_type=jnp.float32).astype(jnp.bfloat16)


def tall(block):
    rows, lanes = block.shape
    return jnp.concatenate([block, jnp.zeros((lanes - rows, lanes), block.dtype)], axis=0)


def prepare_features(t, h, gain_row, weight, k_ref, rhs_ref):
    feats = h.shape[1]
    proj = project(h, gain_row, weight)
    k_ref[t] = proj[:, feats : 2 * feats]
    rhs_ref[t, :, :feats] = proj[:, 2 * feats :]
    return proj[:, :feats]


def prepare_force(t, pos, charge, k_ref, rhs_ref, near_ref):
    feats = charge.shape[1]
    near_ref[t] = pos
    probe = lax.dot_general(
        charge, k_ref[t], (((1,), (1,)), ((), ())), preferred_element_type=jnp.float32
    )
    rows = probe * pos
    high = rows.astype(jnp.bfloat16).astype(jnp.float32)
    columns = tall(jnp.concatenate([high, rows - high], axis=0)).T
    rhs_ref[t, :, feats:] = columns.astype(jnp.bfloat16)


def score_slots(i, group, own, q, pos, slot_of, work, s_ref, falloff):
    k_ref, near_ref = work.k, work.near
    beads, feats = q.shape
    heads = falloff.shape[0]
    lane = lax.broadcasted_iota(jnp.int32, (beads, feats), 1) // (feats // heads)
    zero = jnp.zeros_like(q)
    masked = [jnp.where(lane == e, q, zero) for e in range(heads)]
    chunks = range(0, beads, CHUNK)
    stacked = jnp.concatenate([m[r : r + CHUNK] for r in chunks for m in masked], axis=0)
    columns = tall(pos).T
    rates = [falloff[e] * -LOG2E for e in range(heads)]
    for part in group:
        where = [jnp.where(slot_of(n) >= 0, slot_of(n), own) for n in part]
        present = [(slot_of(n) >= 0).astype(jnp.float32) for n in part]
        keys = join([k_ref[w] for w in where], 0)
        logits = lax.dot_general(
            stacked, keys, (((1,), (1,)), ((), ())), preferred_element_type=jnp.float32
        )
        near = join([near_ref[w] for w in where], 1)
        occupied = join([jnp.full((1, beads), v, jnp.float32) for v in present], 1)
        for r in chunks:
            squared = None
            for c in range(3):
                offset = columns[r : r + CHUNK, c : c + 1] - near[c : c + 1, :]
                squared = offset * offset if squared is None else squared + offset * offset
            squared = jnp.minimum(squared, 1.0)
            window = jnp.full_like(squared, WINDOW[0])
            for coefficient in WINDOW[1:]:
                window = window * squared + coefficient
            window = window * (1.0 - squared)
            window = (window * window * occupied).astype(jnp.bfloat16)
            for e in range(heads):
                start = r * heads + e * CHUNK
                half = logits[start : start + CHUNK]
                act = (half + half * jnp.tanh(half)).astype(jnp.bfloat16)
                decay = jnp.exp2((squared * rates[e]).astype(jnp.bfloat16))
                s_ref[i, start : start + CHUNK, part[0] * beads : (part[-1] + 1) * beads] = act * (
                    window * decay
                )


def finish_tile(i, own, h, pos, noise, scale, slot_of, slot_count, work, s_ref, mixing, out_weight):
    beads, feats = h.shape
    heads = mixing.shape[0]
    lane = lax.broadcasted_iota(jnp.int32, (CHUNK, feats), 1) // (feats // heads)
    where = [jnp.where(slot_of(n) >= 0, slot_of(n), own) for n in range(slot_count)]
    rhs = jnp.concatenate([work.rhs[w] for w in where], axis=0)
    sums = jnp.dot(s_ref[i], rhs, preferred_element_type=jnp.float32)
    messages, pulls = [], []
    for r in range(0, beads, CHUNK):
        message = jnp.zeros((CHUNK, feats), jnp.float32)
        pull = jnp.zeros((CHUNK, feats), jnp.float32)
        for e in range(heads):
            part = sums[r * heads + e * CHUNK : r * heads + (e + 1) * CHUNK]
            message = jnp.where(lane == e, part[:, :feats], message)
            pull = pull + mixing[e] * part[:, feats:]
        messages.append(message)
        pulls.append(pull)
    message = (jnp.concatenate(messages, axis=0) * MESSAGE_SCALE).astype(jnp.bfloat16)
    pulls = jnp.concatenate(pulls, axis=0)
    mixed = jnp.dot(message, out_weight, preferred_element_type=jnp.float32)
    updated = (h.astype(jnp.float32) + mixed).astype(jnp.bfloat16)
    turned = pulls.T
    turned = turned[0:8] + turned[8:16]
    force = (pos * turned[3:4] - turned) * FORCE_SCALE
    moved = pos + DURATION_DELTA * force + (JITTER_SIZE * scale) * noise
    return updated, moved, force


def join(parts, axis):
    return parts[0] if len(parts) == 1 else jnp.concatenate(parts, axis=axis)


def rows_of(ref, a, b, fill):
    rows = [ref[0, c, a, pl.ds(b, 1), :] for c in range(3)]
    beads = rows[0].shape[1]
    rows.append(jnp.full((1, beads), fill, jnp.float32))
    rows.append(jnp.zeros((4, beads), jnp.float32))
    return jnp.concatenate(rows, axis=0)


OPERANDS = 14


class Work:
    def __init__(self, k, rhs, near, q):
        self.k, self.rhs, self.near, self.q = k, rhs, near, q


DIRECTIONS = [(dx, dy) for dx in (-1, 0, 1) for dy in (-1, 0, 1) if (dx, dy) != (0, 0)]


def side(step, size):
    if step == 0:
        return 0, size, 1
    return (size - 1, 1, 0) if step > 0 else (0, 1, size + 1)


def window_kernel(sizes, *refs):
    operands, refs = refs[:OPERANDS], refs[OPERANDS:]
    outs, held, refs = refs[:3], refs[3 : 3 + OPERANDS], refs[3 + OPERANDS :]
    load_sem, refs = refs[0], refs[1:]
    loads = [
        pltpu.make_async_copy(src, dst, load_sem.at[n])
        for n, (src, dst) in enumerate(zip(operands, held))
    ]
    for load in loads:
        load.start()
    window_body(sizes, loads, *held, *outs, *refs)


def window_body(sizes, loads, h_in, p_in, noise1, noise2, slots, levels, heat_slot, partner, gain,
                  weight, out_weight, charge_ref, falloff, mixing, h_out, moved_out, force_out, k_ref,
                  rhs_ref, near_ref, q_ref, s_ref, rim1, rim2, pos1, pos2, mine_h, mine_p, spread_a,
                  spread_b, spread_p, route_h, route_p, trade_h, trade_p, halo_send, halo_recv,
                  swap_send, swap_recv):
    reps, nx, ny = sizes
    _, tx, ty, beads, feats = h_in.shape
    tiles = tx * ty
    ex, ey = tx + 2, ty + 2
    slot_count = slots.shape[2]
    me, gx, gy = lax.axis_index("rep"), lax.axis_index("gx"), lax.axis_index("gy")
    work = Work(k_ref, rhs_ref, near_ref, q_ref)
    spread_h = (spread_a, spread_b)
    groups = len(spread_h)
    piece = tiles * beads // groups // reps
    per = mine_p.shape[1]

    def has(dx, dy):
        conds = []
        if dx:
            conds.append(gx < nx - 1 if dx > 0 else gx > 0)
        if dy:
            conds.append(gy < ny - 1 if dy > 0 else gy > 0)
        return conds[0] if len(conds) == 1 else jnp.logical_and(*conds)

    def other(k):
        return (lax.rem(me + k, reps), gx, gy)

    barrier = pltpu.get_barrier_semaphore()
    for k in range(1, reps):
        pl.semaphore_signal(barrier, inc=1, device_id=other(k), device_id_type=pl.DeviceIdType.MESH)
    for dx, dy in DIRECTIONS:
        @pl.when(has(dx, dy))
        def _(dx=dx, dy=dy):
            pl.semaphore_signal(barrier, inc=1, device_id=(me, gx + dx, gy + dy),
                                device_id_type=pl.DeviceIdType.MESH)

    for load in loads:
        load.wait()
    scale = jnp.sqrt(jnp.full((1, beads), levels[heat_slot[0]], jnp.float32))
    gain_row, weights, out_w = gain[...], weight[...], out_weight[...]
    charge = jnp.broadcast_to(charge_ref[...].astype(jnp.float32), (8, feats)).astype(jnp.bfloat16)

    def prepare_pos(row, col, pos):
        prepare_force(row * ey + col, pos, charge, k_ref, rhs_ref, near_ref)

    def prepare(row, col, h):
        q = prepare_features(row * ey + col, h, gain_row, weights, k_ref, rhs_ref)
        if 1 <= row <= tx and 1 <= col <= ty:
            q_ref[(row - 1) * ty + col - 1] = q * jnp.bfloat16(0.125)

    def halo_copy(step, d, kind, h_src, rim, pos):
        dx, dy = DIRECTIONS[d]
        (r0, nr, r1), (c0, nc, c1) = side(dx, tx), side(dy, ty)
        target = (me, gx + dx, gy + dy)
        if kind == 0:
            src = h_src.at[pl.ds(r0, nr), pl.ds(c0, nc)]
            dst = rim.at[pl.ds(r1, nr), pl.ds(c1, nc)]
        else:
            src = pos.at[pl.ds(r0 + 1, nr), pl.ds(c0 + 1, nc)]
            dst = pos.at[pl.ds(r1, nr), pl.ds(c1, nc)]
        return pltpu.make_async_remote_copy(
            src_ref=src, dst_ref=dst, send_sem=halo_send.at[step, d, kind],
            recv_sem=halo_recv.at[step, d, kind], device_id=target,
            device_id_type=pl.DeviceIdType.MESH)

    def slot_reader(i):
        return lambda n: slots[i // ty, lax.rem(i, ty), n]

    def own_of(i):
        return (i // ty + 1) * ey + lax.rem(i, ty) + 1

    def start_halo(number, kind, h_src, rim, pos):
        for d, (dx, dy) in enumerate(DIRECTIONS):
            @pl.when(has(dx, dy))
            def _(d=d):
                halo_copy(number, d, kind, h_src, rim, pos).start()

    def step(number, h_src, rim, pos, noise, finish, cuts, after_cut):
        def self_body(i, carry):
            score_slots(i, ((0,),), own_of(i), q_ref[i], near_ref[own_of(i)], slot_reader(i), work,
                        s_ref, falloff)
            return carry

        lax.fori_loop(0, tiles, self_body, 0, unroll=True)
        for d, (dx, dy) in enumerate(DIRECTIONS):
            @pl.when(has(-dx, -dy))
            def _(d=d, dx=dx, dy=dy):
                for kind in range(2):
                    halo_copy(number, d, kind, h_src, rim, pos).wait_recv()
                (_, nr, r1), (_, nc, c1) = side(dx, tx), side(dy, ty)
                for row in range(r1, r1 + nr):
                    for col in range(c1, c1 + nc):
                        prepare(row, col, rim[row, col])
                        prepare_pos(row, col, pos[row, col])

        rest = [(n, n + 1) if n + 1 < slot_count else (n,) for n in range(1, slot_count, 2)]

        def body(i, carry):
            a, b = i // ty, lax.rem(i, ty)
            here = near_ref[own_of(i)]
            score_slots(i, rest, own_of(i), q_ref[i], here, slot_reader(i), work, s_ref, falloff)
            finish(i, a, b, *finish_tile(
                i, own_of(i), h_src[a, b], here, rows_of(noise, a, b, 0.0), scale, slot_reader(i),
                slot_count, work, s_ref, mixing, out_w))
            return carry

        for first, last in zip(cuts[:-1], cuts[1:]):
            lax.fori_loop(first, last, body, 0, unroll=2 if (last - first) % 2 == 0 else 1)
            after_cut(last)
        for d, (dx, dy) in enumerate(DIRECTIONS):
            @pl.when(has(dx, dy))
            def _(d=d):
                for kind in range(2):
                    halo_copy(number, d, kind, h_src, rim, pos).wait_send()

    def swap_copy(phase, part, k, src, dst):
        return pltpu.make_async_remote_copy(
            src_ref=src, dst_ref=dst, send_sem=swap_send.at[phase, part, k],
            recv_sem=swap_recv.at[phase, part, k], device_id=other(k),
            device_id_type=pl.DeviceIdType.MESH)

    def first_copy(part, k):
        peer = lax.rem(me + k, reps)
        if part == groups:
            return swap_copy(0, part, k, mine_p.at[peer], spread_p.at[me])
        return swap_copy(0, part, k, mine_h.at[part, peer], spread_h[part].at[me])

    def place(part, owner):
        start = part * (tiles * beads // groups) + owner * piece
        t = start // beads
        return t // ty, lax.rem(t, ty), pl.ds(pl.multiple_of(lax.rem(start, beads), piece), piece)

    def second_copy(part, k):
        if part == groups:
            return swap_copy(1, part, k, route_p.at[k], trade_p.at[me])
        a, b, rows = place(part, me)
        return swap_copy(1, part, k, route_h.at[part, k], trade_h.at[a, b, rows])

    def send_first(part):
        for k in range(1, reps):
            first_copy(part, k).start()
        if part == groups:
            spread_p[me] = mine_p[me]
        else:
            spread_h[part][me] = mine_h[part, me]

    def send_second(part):
        for k in range(1, reps):
            first_copy(part, k).wait_recv()
        for k in range(reps):
            chosen = partner[lax.rem(me + k, reps)]
            if part == groups:
                value = spread_p[chosen]
                if k:
                    route_p[k] = value
                else:
                    trade_p[me] = value
            else:
                value = spread_h[part][chosen]
                if k:
                    route_h[part, k] = value
                else:
                    a, b, rows = place(part, me)
                    trade_h[a, b, rows, :] = value
            if k:
                second_copy(part, k).start()

    def finish_first(i, a, b, updated, moved, force):
        pieces = beads // piece
        for n in range(pieces):
            which = i * pieces + n
            mine_h[which // reps, lax.rem(which, reps)] = updated[n * piece : (n + 1) * piece]
        for c in range(3):
            row = c * tiles + i
            mine_p[row // per, pl.ds(lax.rem(row, per), 1), :] = moved[c : c + 1]

    def after_first(done):
        if done == tiles // groups:
            send_first(0)
        elif done < tiles:
            send_second(0)
        else:
            send_first(groups)
            send_first(1)
            send_second(groups)
            send_second(1)

    def finish_second(i, a, b, updated, moved, force):
        h_out[0, a, b] = updated
        for c in range(3):
            moved_out[0, c, a, pl.ds(b, 1), :] = moved[c : c + 1]
            force_out[0, c, a, pl.ds(b, 1), :] = force[c : c + 1]

    grid = [(a, b) for a in range(tx) for b in range(ty)]
    half_tiles = tiles // groups
    for a, b in grid:
        pos1[a + 1, b + 1] = rows_of(p_in, a, b, 1.0)
    for a, b in grid[:half_tiles]:
        prepare(a + 1, b + 1, h_in[0, a, b])
    mine_p[...] = jnp.zeros_like(mine_p)

    columns = 1 + jnp.minimum(gx, 1) + jnp.minimum(nx - 1 - gx, 1)
    lines = 1 + jnp.minimum(gy, 1) + jnp.minimum(ny - 1 - gy, 1)
    pl.semaphore_wait(barrier, reps - 2 + columns * lines)

    for kind in range(2):
        start_halo(0, kind, h_in.at[0], rim1, pos1)
    for a, b in grid[half_tiles:]:
        prepare(a + 1, b + 1, h_in[0, a, b])
    for a, b in grid:
        prepare_pos(a + 1, b + 1, rows_of(p_in, a, b, 1.0))
    cuts = (0, half_tiles, tiles - 1, tiles)
    step(0, h_in.at[0], rim1, pos1, noise1, finish_first, cuts, after_first)

    def arrive(part):
        for k in range(1, reps):
            second_copy(part, k).wait_recv()

    arrive(0)
    for a, b in grid[:half_tiles]:
        prepare(a + 1, b + 1, trade_h[a, b])
    arrive(groups)
    for a, b in grid:
        rows = []
        for c in range(3):
            row = c * tiles + a * ty + b
            rows.append(trade_p[row // per, row % per : row % per + 1, :])
        rows.append(jnp.full((1, beads), 1.0, jnp.float32))
        rows.append(jnp.zeros((4, beads), jnp.float32))
        pos2[a + 1, b + 1] = jnp.concatenate(rows, axis=0)
    start_halo(1, 1, trade_h, rim2, pos2)
    arrive(1)
    start_halo(1, 0, trade_h, rim2, pos2)
    for a, b in grid[half_tiles:]:
        prepare(a + 1, b + 1, trade_h[a, b])
    for a, b in grid:
        prepare_pos(a + 1, b + 1, pos2[a + 1, b + 1])
    step(1, trade_h, rim2, pos2, noise2, finish_second, (0, tiles), lambda done: None)
    for part in range(groups + 1):
        for k in range(1, reps):
            first_copy(part, k).wait_send()
            second_copy(part, k).wait_send()


def per_device(
    particle_descriptors,
    particle_locations_all,
    earlier_jitter,
    later_jitter,
    adjacent_tile_slots,
    thermal_levels,
    heat_slot_of_copy,
    partner_choice,
    normalizer_gain,
    query_lookup_matrix,
    message_output_matrix,
    lookup_charge_map,
    attention_head_falloff,
    attention_head_weight,
):
    _, tx, ty, beads, feats = particle_descriptors.shape
    reps, nx, ny = (lax.axis_size(axis) for axis in ("rep", "gx", "gy"))
    tiles, ext = tx * ty, (tx + 2) * (ty + 2)
    heads = attention_head_falloff.shape[0]
    slot_count = adjacent_tile_slots.shape[2]
    groups = 2
    piece = tiles * beads // groups // reps
    per = -(-3 * tiles // reps)
    vmem = pl.BlockSpec(memory_space=pltpu.VMEM)
    bf16, f32 = jnp.bfloat16, jnp.float32
    operands = (
        particle_descriptors,
        particle_locations_all,
        earlier_jitter,
        later_jitter,
        adjacent_tile_slots,
        thermal_levels,
        heat_slot_of_copy,
        partner_choice,
        normalizer_gain.reshape(1, feats),
        query_lookup_matrix,
        message_output_matrix,
        lookup_charge_map.reshape(1, feats),
        attention_head_falloff,
        attention_head_weight,
    )
    return pl.pallas_call(
        functools.partial(window_kernel, (reps, nx, ny)),
        out_shape=(
            jax.ShapeDtypeStruct(particle_descriptors.shape, bf16),
            jax.ShapeDtypeStruct(particle_locations_all.shape, f32),
            jax.ShapeDtypeStruct(particle_locations_all.shape, f32),
        ),
        in_specs=[pl.BlockSpec(memory_space=pltpu.HBM)] * OPERANDS,
        out_specs=(vmem, vmem, vmem),
        scratch_shapes=[
            (pltpu.SMEM if n in (4, 5, 6, 7, 12, 13) else pltpu.VMEM)(x.shape, x.dtype)
            for n, x in enumerate(operands)
        ]
        + [
            pltpu.SemaphoreType.DMA((OPERANDS,)),
            pltpu.VMEM((ext, beads, feats), bf16),
            pltpu.VMEM((ext, beads, 2 * feats), bf16),
            pltpu.VMEM((ext, 8, beads), f32),
            pltpu.VMEM((tiles, beads, feats), bf16),
            pltpu.VMEM((tiles, heads * beads, slot_count * beads), bf16),
            pltpu.VMEM((tx + 2, ty + 2, beads, feats), bf16),
            pltpu.VMEM((tx + 2, ty + 2, beads, feats), bf16),
            pltpu.VMEM((tx + 2, ty + 2, 8, beads), f32),
            pltpu.VMEM((tx + 2, ty + 2, 8, beads), f32),
            pltpu.VMEM((groups, reps, piece, feats), bf16),
            pltpu.VMEM((reps, per, beads), f32),
            pltpu.VMEM((reps, piece, feats), bf16),
            pltpu.VMEM((reps, piece, feats), bf16),
            pltpu.VMEM((reps, per, beads), f32),
            pltpu.VMEM((groups, reps, piece, feats), bf16),
            pltpu.VMEM((reps, per, beads), f32),
            pltpu.VMEM((tx, ty, beads, feats), bf16),
            pltpu.VMEM((reps, per, beads), f32),
            pltpu.SemaphoreType.DMA((2, len(DIRECTIONS), 2)),
            pltpu.SemaphoreType.DMA((2, len(DIRECTIONS), 2)),
            pltpu.SemaphoreType.DMA((2, groups + 1, reps)),
            pltpu.SemaphoreType.DMA((2, groups + 1, reps)),
        ],
        compiler_params=pltpu.CompilerParams(
            collective_id=0, has_side_effects=True, vmem_limit_bytes=60 * 2**20
        ),
    )(*operands)


def solution(mesh):
    in_specs = (
        P("rep", "gx", "gy", None, None),
        P("rep", None, "gx", "gy", None),
        P("rep", None, "gx", "gy", None),
        P("rep", None, "gx", "gy", None),
        P("gx", "gy", None),
        P(),
        P("rep"),
        P(),
        P(),
        P(),
        P(),
        P(),
        P(),
        P(),
    )
    out_specs = (
        P("rep", "gx", "gy", None, None),
        P("rep", None, "gx", "gy", None),
        P("rep", None, "gx", "gy", None),
    )
    return jax.shard_map(
        per_device, mesh=mesh, in_specs=in_specs, out_specs=out_specs, check_vma=False
    )
```
